128 devices in a mesh: node: 32 (over z, y, core), local: 4 (over x).
Axes of the slice: x: 4, y: 4, z: 4, core: 2. Of those that a mesh axis runs over, the one named last changes fastest.
Arguments:
- tokens: bfloat16 [3072, 7168], P('node'), may hold values from -6 to 6
- routes: int32 [3072, 8], P('node'), may hold values from 0 to 31, all different within a row; in each aligned block of 96 rows (0 to 95, 96 to 191, ...) at most 30 rows name the same one
- route_weight: int32 [3072, 8], P('node'), may hold values from 16 to 1024
- expert_gate: bfloat16 [32, 7168, 2048], P('node', None, 'local'), may hold values from -0.0625 to 0.0625
- expert_up: bfloat16 [32, 7168, 2048], P('node', None, 'local'), may hold values from -0.0625 to 0.0625
- expert_down: bfloat16 [32, 2048, 7168], P('node', 'local'), may hold values from -0.125 to 0.125
Outputs:
- mixed: bfloat16 [3072, 7168], P('node')
The draws below stay inside these ranges and needn't reach their ends.
Inputs may be any that keep to these rules, and one draw needn't show every extreme that they name: `routes`: the 8 experts of a token are distinct. Among the 96 rows of one node no expert is named more than 30 times, and in every draw some node names some expert exactly 30 times.
All inputs are finite; a program needn't handle non-finite values.
Results may differ from the reference program's by a relative error of at most 0.015.
Values may be sent and summed in bfloat16 or wider, within the bound.
A program may use at most 128 MiB of HBM per device.

```python
import math
import jax
import jax.numpy as jnp
import numpy as np
from jax import lax

D = 7168
FF = 2048
EXPERTS = 32
TOPK = 8
TOK_NODE = 96
CAP = 30
TOKENS = 3072
N_NODE = 32
N_LOCAL = 4


def plant(values, rng, smallest, top_value):
    longest = values.shape.index(max(values.shape))
    spots = []
    for shift in (0, 1):
        where = [jax.random.randint(jax.random.fold_in(rng, axis), (), 0, length) for axis, length in enumerate(values.shape)]
        where[longest] = (where[longest] + shift) % values.shape[longest]
        spots.append(tuple(where))
    return values.at[spots[0]].set(smallest).at[spots[1]].set(top_value)


def block_scale(own_key, dims, shards, low, top_value):
    def one(dim, parts):
        heights = jax.random.uniform(jax.random.fold_in(jax.random.fold_in(own_key, 6), dim), (parts,), jnp.float32, low / len(shards), top_value / len(shards))
        return jnp.repeat(jnp.exp(heights), dims[dim] // parts).reshape((-1,) + (1,) * (len(dims) - dim - 1))

    factor_of = one(*shards[0])
    for cut in shards[1:]:
        factor_of = factor_of * one(*cut)
    return factor_of


def assign_block(rng, own, number, rows, count, top, most, skew):
    sequence = jax.random.permutation(rng, count)
    heavy_load, usual = shares(count, rows * top, most, skew, True), shares(count, rows * top, most, skew, False)
    places = jnp.arange(count)

    def named(tallies, turn):
        used = int((tallies > 0).sum())
        fixed = max(1, used // 4)
        shifted = fixed + (places - fixed + turn * (used - fixed)) % max(1, count - fixed)
        return jnp.zeros((count,), jnp.int32).at[sequence[jnp.where(places < fixed, places, shifted)]].set(jnp.asarray(tallies, jnp.int32))

    tallies = jnp.where(number % 4 == 0, named(heavy_load, number // 4), named(usual, number - number // 4 - 1))
    mixed = jax.random.permutation(jax.random.fold_in(own, 3), count)
    giver, taker = mixed[0:count // 2 * 2:2], mixed[1:count // 2 * 2:2]
    slack = jnp.minimum(tallies[giver] - 1, most - tallies[taker]) // 2
    slack = jnp.where((giver == sequence[0]) | (taker == sequence[0]) | (tallies[taker] == 0), 0, jnp.maximum(slack, 0))
    shifted = jax.random.randint(jax.random.fold_in(own, 4), (count // 2,), 0, 1 << 20) % (slack + 1)
    tallies = tallies.at[giver].add(-shifted).at[taker].add(shifted)
    items = jnp.searchsorted(jnp.cumsum(tallies), jnp.arange(rows * top), side="right").astype(jnp.int32)
    listing = items.reshape(top, rows).T
    listing = listing[jax.random.permutation(jax.random.fold_in(own, 1), rows)]
    turn = jax.random.randint(jax.random.fold_in(own, 2), (rows, 1), 0, top)
    return jnp.take_along_axis(listing, (jnp.arange(top)[None, :] + turn) % top, axis=1)


def shares(amount, total, reach, skew, full):
    loads = [(1 << 20) // math.isqrt(standing ** skew) + 1 for standing in range(1, amount + 1)]
    largest = reach if full else min(reach, max(-(-total // amount), total * loads[0] // sum(loads)))
    least = 1 if total - largest >= amount - 1 else 0
    holding, surplus = [largest] + [least] * (amount - 1), total - largest - least * (amount - 1)
    while surplus > 0:
        candidates = [i for i in range(1, amount) if holding[i] < largest] or [i for i in range(1, amount) if holding[i] < reach]
        pool, left = sum([loads[i] for i in candidates]), surplus
        for i in candidates:
            more = min(reach - holding[i], max(1, left * loads[i] // pool), surplus)
            holding[i] = holding[i] + more
            surplus = surplus - more
    return np.array(holding)


def normal_values(rng, dims, width, bound, split=(), kind=jnp.bfloat16):
    array = width * jax.random.normal(rng, dims, jnp.float32)
    if split:
        array = array * block_scale(rng, dims, split, -0.22, 0.18)
    return jnp.clip(array, -bound, bound).astype(kind)


def setup_inputs(seed: int = 0) -> dict:
    key_list = jax.random.split(jax.random.key(seed), 7)
    tokens = normal_values(key_list[0], (TOKENS, D), 1.0, 6.0, ((0, 32),))
    routes_keys = jax.random.split(jax.random.fold_in(key_list[1], 1), TOKENS // TOK_NODE)
    routes_turns = jax.random.permutation(jax.random.fold_in(key_list[1], 3), TOKENS // TOK_NODE)
    routes = jax.vmap(lambda own, number: assign_block(jax.random.fold_in(key_list[1], 2), own, number, TOK_NODE, EXPERTS, TOPK, CAP, 2))(routes_keys, routes_turns).reshape((TOKENS, TOPK))
    route_weight = plant(jax.random.randint(key_list[2], (TOKENS, TOPK), 16, 1025), jax.random.fold_in(key_list[2], 1), 16, 1024).astype(jnp.int32)
    expert_gate = normal_values(key_list[3], (EXPERTS, D, FF), D ** -0.5, 0.0625, ((0, 32), (2, 4)))
    expert_up = normal_values(key_list[4], (EXPERTS, D, FF), D ** -0.5, 0.0625, ((0, 32), (2, 4)))
    expert_down = normal_values(key_list[5], (EXPERTS, FF, D), FF ** -0.5, 0.125, ((0, 32), (1, 4)))
    return dict(tokens=tokens, routes=routes, route_weight=route_weight, expert_gate=expert_gate, expert_up=expert_up, expert_down=expert_down)


def ffn_quarters(rows, gate, up, down):
    values = rows.astype(jnp.float32)
    gate_out = jnp.dot(values, gate.astype(jnp.float32), precision=lax.Precision.HIGHEST)
    up_out = jnp.dot(values, up.astype(jnp.float32), precision=lax.Precision.HIGHEST)
    hidden = lax.optimization_barrier((jax.nn.silu(gate_out) * up_out).astype(jnp.bfloat16)).astype(jnp.float32)
    quarter = gate.shape[1] // N_LOCAL
    total = jnp.zeros((rows.shape[0], down.shape[1]), jnp.float32)
    for index in range(N_LOCAL):
        part = jnp.dot(hidden[:, index * quarter:(index + 1) * quarter],
                       down[index * quarter:(index + 1) * quarter].astype(jnp.float32),
                       precision=lax.Precision.HIGHEST)
        total = total + lax.optimization_barrier(part.astype(jnp.bfloat16)).astype(jnp.float32)
    return total


def reference(tokens, routes, route_weight, expert_gate, expert_up, expert_down):
    blocks = N_NODE
    flat = routes.reshape(blocks, TOK_NODE * TOPK)
    labels = jnp.arange(EXPERTS, dtype=jnp.int32)
    onehot = (flat[:, :, None] == labels[None, None, :]).astype(jnp.int32)
    before = jnp.cumsum(onehot, axis=1) - onehot
    slot = jnp.sum(before * onehot, axis=2).astype(jnp.int32)
    block_id = jnp.arange(blocks, dtype=jnp.int32)[:, None]
    place = block_id * CAP + slot
    pair_id = jnp.arange(TOK_NODE * TOPK, dtype=jnp.int32)[None, :]
    token_id = block_id * TOK_NODE + pair_id // TOPK
    index = jnp.full((EXPERTS, blocks * CAP), TOKENS, jnp.int32)
    index = index.at[flat.reshape(-1), place.reshape(-1)].set(token_id.reshape(-1).astype(jnp.int32))
    scales = jnp.zeros((EXPERTS, blocks * CAP), jnp.float32)
    scales = scales.at[flat.reshape(-1), place.reshape(-1)].set(route_weight.reshape(-1).astype(jnp.float32) / 1024.0)
    padded = jnp.concatenate([tokens, jnp.zeros((1, D), jnp.bfloat16)], axis=0)

    def one_expert(total, item):
        rows_index, weights, gate, up, down = item
        rows = padded[rows_index]
        result = ffn_quarters(rows, gate, up, down)
        result = lax.optimization_barrier(result.astype(jnp.bfloat16)).astype(jnp.float32)
        total = total.at[rows_index].add(weights[:, None] * result)
        return total, None

    start = jnp.zeros((TOKENS + 1, D), jnp.float32)
    total, unused = lax.scan(one_expert, start, (index, scales, expert_gate, expert_up, expert_down))
    return total[:TOKENS].astype(jnp.bfloat16)
```

```python
import jax
import jax.numpy as jnp
from jax import lax
from jax.experimental import pallas as pl
from jax.experimental.pallas import tpu as pltpu
from jax.sharding import PartitionSpec as P

EXPERTS = 32
SLOTS = 32
NODES = 32
ROWS = NODES * SLOTS
D = 7168
HALF = D // 2
QUARTER = D // 4
HID = 512
TOK = 96
CHUNKS = 7
PART = QUARTER // CHUNKS
WIDE = 2 * PART
TILE = 256
MESH = pl.DeviceIdType.MESH
MIB = 1 << 20


def peer(node, step):
    step = lax.rem(step * 11, 32)
    core, y, z = lax.rem(node, 2), lax.rem(node // 2, 4), node // 8
    core = lax.rem(core + lax.rem(step, 2), 2)
    y = lax.rem(y + lax.rem(step // 2, 4), 4)
    z = lax.rem(z + step // 8, 4)
    return (z * 4 + y) * 2 + core


def block_of(index):
    return pl.ds(pl.multiple_of(index * SLOTS, SLOTS), SLOTS)


def columns(start, size):
    return pl.ds(pl.multiple_of(start, 128), size)


def drain(ref, sem):
    pltpu.make_async_copy(ref, ref, sem).wait()


def spread(src, dst, chunk, node, x, send_sem, recv_sem):
    mine = block_of(node)

    @pl.loop(1, NODES)
    def _(step):
        to = peer(node, step)
        pltpu.make_async_remote_copy(
            src_ref=src.at[chunk, block_of(to)],
            dst_ref=dst.at[chunk, mine],
            send_sem=send_sem.at[chunk],
            recv_sem=recv_sem.at[chunk],
            device_id=(to, x),
            device_id_type=MESH,
        ).start()

    pltpu.make_async_copy(src.at[chunk, mine], dst.at[chunk, mine], recv_sem.at[chunk]).start()


def drain_spread(dst, chunk, send_sem):
    part = dst.at[chunk, pl.ds(0, ROWS - SLOTS)]
    drain(part, send_sem.at[chunk])


def greet(node, x, others):
    barrier = pltpu.get_barrier_semaphore()

    @pl.loop(1, NODES)
    def _(step):
        pl.semaphore_signal(barrier, inc=1, device_id=(peer(node, step), x), device_id_type=MESH)

    for other in others:
        pl.semaphore_signal(barrier, inc=1, device_id=(node, other), device_id_type=MESH)
    pl.semaphore_wait(barrier, NODES - 1 + len(others))


def dispatch_kernel(
    select, tokens, gate, up, hidden,
    outbound, direct, passed, weights, total,
    send_sem, recv_sem, pass_send, pass_recv, weight_sem,
):
    node, x = lax.axis_index("node"), lax.axis_index("local")
    right, left = lax.rem(x + 1, 4), lax.rem(x + 3, 4)
    side = lax.rem(x, 2)

    @pl.loop(0, CHUNKS)
    def _(p):
        for k in range(2):
            base = (side if k == 0 else 1 - side) * HALF + p * PART
            for q in range(2):
                for m, source in enumerate((gate, up)):
                    pltpu.make_async_copy(
                        source.at[0, pl.ds(pl.multiple_of(base + q * QUARTER, PART), PART)],
                        weights.at[k, p, pl.ds(q * PART, PART), pl.ds(m * HID, HID)],
                        weight_sem.at[k, p],
                    ).start()

    greet(node, x, (left, right))

    @pl.loop(0, CHUNKS)
    def _(p):
        base = side * HALF + p * PART

        @pl.loop(0, ROWS // TILE)
        def _(t):
            rows = pl.ds(pl.multiple_of(t * TILE, TILE), TILE)
            for q in range(2):
                outbound[p, rows, pl.ds(q * PART, PART)] = jnp.dot(
                    select[rows, :],
                    tokens[:, columns(base + q * QUARTER, PART)],
                    preferred_element_type=jnp.float32,
                ).astype(jnp.bfloat16)

        spread(outbound, direct, p, node, x, send_sem, recv_sem)

    total[...] = jnp.zeros_like(total)

    def add_product(rows_ref, k, p):
        @pl.loop(0, ROWS // TILE)
        def _(t):
            rows = pl.ds(pl.multiple_of(t * TILE, TILE), TILE)
            for m in range(2):
                cols = pl.ds(m * HID, HID)
                total[rows, cols] += jnp.dot(
                    rows_ref[p, rows, :], weights[k, p, :, cols], preferred_element_type=jnp.float32
                )

    def take_passed(p):
        drain(passed.at[p], pass_recv.at[p])
        drain(weights.at[1, p], weight_sem.at[1, p])
        add_product(passed, 1, p)

    @pl.loop(0, CHUNKS)
    def _(p):
        drain(direct.at[p], recv_sem.at[p])
        for q, to in ((0, right), (1, left)):
            part = pl.ds(q * PART, PART)
            pltpu.make_async_remote_copy(
                src_ref=direct.at[p, :, part],
                dst_ref=passed.at[p, :, part],
                send_sem=pass_send.at[p],
                recv_sem=pass_recv.at[p],
                device_id=(node, to),
                device_id_type=MESH,
            ).start()
        drain(weights.at[0, p], weight_sem.at[0, p])
        add_product(direct, 0, p)

        @pl.when(p > 0)
        def _():
            take_passed(p - 1)

    take_passed(CHUNKS - 1)

    @pl.loop(0, ROWS // TILE)
    def _(t):
        rows = pl.ds(pl.multiple_of(t * TILE, TILE), TILE)
        g = total[rows, pl.ds(0, HID)]
        u = total[rows, pl.ds(HID, HID)]
        hidden[rows, :] = (g / (1.0 + jnp.exp(-g)) * u).astype(jnp.bfloat16)

    @pl.loop(0, CHUNKS)
    def _(p):
        drain(direct.at[p], pass_send.at[p])
        drain_spread(direct, p, send_sem)


def return_kernel(
    hidden, down, combine, out,
    across, crossed, outbound, home, mixed,
    cross_send, cross_recv, send_sem, recv_sem, mix_send, mix_recv,
):
    node, x = lax.axis_index("node"), lax.axis_index("local")
    right, left, far = lax.rem(x + 1, 4), lax.rem(x + 3, 4), lax.rem(x + 2, 4)
    side = lax.rem(x, 2)

    greet(node, x, (left, right, far))

    def cross(p):
        base = (1 - side) * HALF + p * PART

        @pl.loop(0, ROWS // TILE)
        def _(t):
            rows = pl.ds(pl.multiple_of(t * TILE, TILE), TILE)
            for q in range(2):
                across[p, rows, pl.ds(q * PART, PART)] = jnp.dot(
                    hidden[rows, :], down[0, :, columns(base + q * QUARTER, PART)],
                    preferred_element_type=jnp.float32,
                ).astype(jnp.bfloat16)

        for q, to in ((0, left), (1, right)):
            part = pl.ds(q * PART, PART)
            pltpu.make_async_remote_copy(
                src_ref=across.at[p, :, part],
                dst_ref=crossed.at[p, :, part],
                send_sem=cross_send.at[p],
                recv_sem=cross_recv.at[p],
                device_id=(node, to),
                device_id_type=MESH,
            ).start()

    def mix(p):
        drain(home.at[p], recv_sem.at[p])
        both = jnp.dot(combine[...], home[p], preferred_element_type=jnp.float32)
        mixed[0, p] = (both[:TOK] + both[TOK:]).astype(jnp.bfloat16)
        for k, to in ((1, left), (2, right), (3, far)):
            pltpu.make_async_remote_copy(
                src_ref=mixed.at[0, p],
                dst_ref=mixed.at[k, p],
                send_sem=mix_send.at[k, p],
                recv_sem=mix_recv.at[k, p],
                device_id=(node, to),
                device_id_type=MESH,
            ).start()

    cross(0)
    cross(1)

    @pl.loop(0, CHUNKS)
    def _(p):
        @pl.when(p + 2 < CHUNKS)
        def _():
            cross(p + 2)

        base = side * HALF + p * PART
        drain(crossed.at[p], cross_recv.at[p])

        @pl.loop(0, ROWS // TILE)
        def _(t):
            rows = pl.ds(pl.multiple_of(t * TILE, TILE), TILE)
            for q in range(2):
                part = pl.ds(q * PART, PART)
                own = jnp.dot(
                    hidden[rows, :], down[0, :, columns(base + q * QUARTER, PART)],
                    preferred_element_type=jnp.float32,
                )
                outbound[p, rows, part] = (own + crossed[p, rows, part].astype(jnp.float32)).astype(jnp.bfloat16)

        spread(outbound, home, p, node, x, send_sem, recv_sem)

        @pl.when(p > 0)
        def _():
            mix(p - 1)

    mix(CHUNKS - 1)

    @pl.loop(0, CHUNKS)
    def _(p):
        for k in range(1, 4):
            drain(mixed.at[k, p], mix_recv.at[k, p])
        mine = mixed[0, p].astype(jnp.float32) + mixed[3, p].astype(jnp.float32)
        other = mixed[1, p].astype(jnp.float32) + mixed[2, p].astype(jnp.float32)
        for q in range(2):
            part = slice(q * PART, (q + 1) * PART)
            start = q * QUARTER + p * PART
            out[:, columns(side * HALF + start, PART)] = mine[:, part].astype(jnp.bfloat16)
            out[:, columns((1 - side) * HALF + start, PART)] = other[:, part].astype(jnp.bfloat16)

    @pl.loop(0, CHUNKS)
    def _(p):
        drain(across.at[p], cross_send.at[p])
        drain_spread(home, p, send_sem)
        for k in range(1, 4):
            drain(mixed.at[k, p], mix_send.at[k, p])


def local(tokens, routes, route_weight, expert_gate, expert_up, expert_down):
    topk = routes.shape[1]
    flat = routes.reshape(-1)
    labels = jnp.arange(EXPERTS, dtype=jnp.int32)
    onehot = (flat[:, None] == labels[None, :]).astype(jnp.int32)
    before = jnp.cumsum(onehot, axis=0) - onehot
    slot = jnp.sum(before * onehot, axis=1)
    target = (flat * SLOTS + slot).reshape(TOK, topk)
    places = jnp.arange(ROWS, dtype=jnp.int32)
    select = jnp.any(target[None, :, :] == places[:, None, None], axis=2).astype(jnp.bfloat16)
    units = jnp.sum(jnp.where(target[:, :, None] == places, route_weight[:, :, None], 0), axis=1)
    low = units & 7
    combine = jnp.concatenate([units - low, low], axis=0).astype(jnp.float32) * (1.0 / 1024.0)
    combine = combine.astype(jnp.bfloat16)

    vmem = pl.BlockSpec(memory_space=pltpu.VMEM)
    anywhere = pl.BlockSpec(memory_space=pl.ANY)
    dma = pltpu.SemaphoreType.DMA
    chunked = pltpu.VMEM((CHUNKS, ROWS, WIDE), jnp.bfloat16)
    hidden = pl.pallas_call(
        dispatch_kernel,
        out_shape=jax.ShapeDtypeStruct((ROWS, HID), jnp.bfloat16),
        in_specs=[vmem, vmem, anywhere, anywhere],
        out_specs=vmem,
        scratch_shapes=[
            chunked, chunked, chunked,
            pltpu.VMEM((2, CHUNKS, WIDE, 2 * HID), jnp.bfloat16),
            pltpu.VMEM((ROWS, 2 * HID), jnp.float32),
            dma((CHUNKS,)), dma((CHUNKS,)), dma((CHUNKS,)), dma((CHUNKS,)), dma((2, CHUNKS)),
        ],
        compiler_params=pltpu.CompilerParams(
            collective_id=0, has_side_effects=True, vmem_limit_bytes=52 * MIB
        ),
        name="dispatch",
    )(select, tokens, expert_gate, expert_up)
    return pl.pallas_call(
        return_kernel,
        out_shape=jax.ShapeDtypeStruct((TOK, D), jnp.bfloat16),
        in_specs=[vmem, vmem, vmem],
        out_specs=vmem,
        scratch_shapes=[
            chunked, chunked, chunked, chunked,
            pltpu.VMEM((4, CHUNKS, TOK, WIDE), jnp.bfloat16),
            dma((CHUNKS,)), dma((CHUNKS,)), dma((CHUNKS,)), dma((CHUNKS,)), dma((4, CHUNKS)), dma((4, CHUNKS)),
        ],
        compiler_params=pltpu.CompilerParams(
            collective_id=1, has_side_effects=True, vmem_limit_bytes=52 * MIB
        ),
        name="give_back",
    )(hidden, expert_down, combine)


def solution(mesh):
    return jax.shard_map(
        local,
        mesh=mesh,
        in_specs=(
            P("node", None),
            P("node", None),
            P("node", None),
            P("node", None, "local"),
            P("node", None, "local"),
            P("node", "local", None),
        ),
        out_specs=P("node", None),
        check_vma=False,
    )
```

```python
import jax
import jax.numpy as jnp
from jax import lax
from jax.experimental import pallas as pl
from jax.experimental.pallas import tpu as pltpu
from jax.sharding import PartitionSpec as P

EXPERTS = 32
SLOTS = 32
ROWS = 32 * SLOTS
D = 7168
HALF = D // 2
QUARTER = D // 4
HID = 512
TOK = 96
TOPK = 8
LANES = 128
UNITS = 7
PART = QUARTER // UNITS
SWAP_OUT = 6
SWAP_BACK = 5
PLANE = 8 * SLOTS
SHIFT = 11
MESH = pl.DeviceIdType.MESH
MIB = 1 << 20


def columns(start):
    return pl.ds(pl.multiple_of(start, PART), PART)


def drain(ref, sem):
    pltpu.make_async_copy(ref, ref, sem).wait()


def remote(src, dst, send_sem, recv_sem, node, x):
    pltpu.make_async_remote_copy(
        src_ref=src, dst_ref=dst, send_sem=send_sem, recv_sem=recv_sem,
        device_id=(node, x), device_id_type=MESH,
    ).start()


class Place:
    def __init__(self):
        self.node, self.x = lax.axis_index("node"), lax.axis_index("local")
        self.core = lax.rem(self.node, 2)
        self.y = lax.rem(self.node // 2, 4)
        self.z = self.node // 8
        self.right, self.left = lax.rem(self.x + 1, 4), lax.rem(self.x + 3, 4)
        self.far = lax.rem(self.x + 2, 4)
        self.side = lax.rem(self.x, 2)

    def at(self, z, y, core):
        return (z * 4 + y) * 2 + core

    def along(self, q, step):
        if q == 0:
            index = lax.rem(self.z + step, 4)
            return index, self.at(index, self.y, self.core)
        index = lax.rem(self.y + step, 4)
        return index, self.at(self.z, index, self.core)

    def across(self, q, step):
        core = lax.rem(self.core + lax.rem(step, 2), 2)
        if q == 0:
            index = lax.rem(self.y + step // 2, 4)
            return index, core, self.at(self.z, index, core)
        index = lax.rem(self.z + step // 2, 4)
        return index, core, self.at(index, self.y, core)

    def own(self, q):
        return self.z if q == 0 else self.y

    def base(self, j):
        return jnp.where(j < UNITS, self.side * HALF + j * PART, (1 - self.side) * HALF + (j - UNITS) * PART)

    def plane_targets(self, q):
        row = lax.broadcasted_iota(jnp.int32, (PLANE, LANES), 0)
        if q == 0:
            return row + self.z * PLANE
        return ((row >> 6) * 8 + self.y * 2 + ((row >> 5) & 1)) * SLOTS + (row & (SLOTS - 1))

    def greet(self, others):
        barrier = pltpu.get_barrier_semaphore()

        def hello(node, x):
            pl.semaphore_signal(barrier, inc=1, device_id=(node, x), device_id_type=MESH)

        for step in range(1, 8):
            hello(self.across(0, step)[2], self.x)
        for step in range(2, 8):
            hello(self.across(1, step)[2], self.x)
        for other in others:
            hello(self.node, other)
        pl.semaphore_wait(barrier, 13 + len(others))


def unit_of(i, swapped):
    return jnp.where(i < UNITS, i, i + swapped)


def dispatch_kernel(
    code, tokens, gate, up, hidden, codes_out,
    codes, select, staged, outbound, direct, passed, weights, total,
    code_send, code_recv, stage_send, stage_recv, send_sem, recv_sem, pass_send, pass_recv, weight_sem,
):
    me = Place()
    straight = direct.shape[0]

    @pl.loop(0, 2 * UNITS)
    def _(j):
        for q in range(2):
            for m, source in enumerate((gate, up)):
                pltpu.make_async_copy(
                    source.at[0, columns(me.base(j) + q * QUARTER)],
                    weights.at[j, pl.ds(q * PART, PART), pl.ds(m * HID, HID)],
                    weight_sem.at[j],
                ).start()

    me.greet((me.left, me.right))

    def stage(i):
        base = me.base(unit_of(i, SWAP_OUT))
        for step in range(1, 4):
            for q in range(2):
                remote(
                    tokens.at[:, columns(base + q * QUARTER)], staged.at[i, q, me.own(q)],
                    stage_send.at[i], stage_recv.at[i], me.along(q, step)[1], me.x,
                )
        for q in range(2):
            pltpu.make_async_copy(
                tokens.at[:, columns(base + q * QUARTER)], staged.at[i, q, me.own(q)], stage_recv.at[i]
            ).start()

    for q in range(2):
        for step in range(1, 4):
            remote(code, codes.at[q, me.own(q)], code_send, code_recv, me.along(q, step)[1], me.x)
        pltpu.make_async_copy(code, codes.at[q, me.own(q)], code_recv).start()
    stage(0)
    stage(1)
    total[...] = jnp.zeros_like(total)
    drain(codes, code_recv)
    codes_out[...] = codes[...]
    for q in range(2):
        wanted = me.plane_targets(q)
        for s in range(4):
            have = codes[q, s] >> SHIFT
            hit = have[0:1] == wanted
            for k in range(1, TOPK):
                hit = hit | (have[k:k + 1] == wanted)
            select[q, s] = hit.astype(jnp.float32).astype(jnp.bfloat16)

    def pick(i):
        drain(staged.at[i], stage_recv.at[i])
        for q in range(2):
            for s in range(4):
                outbound[i, q, :, s] = jnp.dot(
                    select[q, s, :, :TOK], staged[i, q, s], preferred_element_type=jnp.float32
                ).astype(jnp.bfloat16).reshape(8, SLOTS, PART)

        @pl.loop(1, 8)
        def _(step):
            index, core, node = me.across(0, step)
            remote(
                outbound.at[i, 0, index * 2 + core], direct.at[i, 0, me.core, :, me.y],
                send_sem.at[i], recv_sem.at[i], node, me.x,
            )
            index, core, node = me.across(1, step)
            remote(
                outbound.at[i, 1, index * 2 + core], direct.at[i, 1, me.core, me.z],
                send_sem.at[i], recv_sem.at[i], node, me.x,
            )

        pltpu.make_async_copy(
            outbound.at[i, 0, me.y * 2 + me.core], direct.at[i, 0, me.core, :, me.y], recv_sem.at[i]
        ).start()
        pltpu.make_async_copy(
            outbound.at[i, 1, me.z * 2 + me.core], direct.at[i, 1, me.core, me.z], recv_sem.at[i]
        ).start()

    def add_product(rows_ref, i, j):
        drain(weights.at[j], weight_sem.at[j])

        @pl.loop(0, 4)
        def _(t):
            core, z = t // 2, lax.rem(t, 2) * 2
            rows = pl.ds(pl.multiple_of(t * 256, 256), 256)
            left = jnp.concatenate(
                [rows_ref[i, q, core, pl.ds(z, 2)].reshape(256, PART) for q in range(2)], axis=1
            )
            for m in range(2):
                cols = pl.ds(m * HID, HID)
                total[rows, cols] += jnp.dot(left, weights[j, :, cols], preferred_element_type=jnp.float32)

    def take_direct(i):
        drain(direct.at[i], recv_sem.at[i])

        @pl.when(i < SWAP_OUT)
        def _():
            for q, to in ((0, me.right), (1, me.left)):
                remote(direct.at[i, q], passed.at[i, q], pass_send.at[i], pass_recv.at[i], me.node, to)

        add_product(direct, i, unit_of(i, SWAP_OUT))

    def take_passed(i):
        drain(passed.at[i], pass_recv.at[i])
        add_product(passed, i, UNITS + i)

    @pl.loop(0, straight + 1)
    def _(i):
        @pl.when(i + 2 < straight)
        def _():
            stage(i + 2)

        @pl.when(i < straight)
        def _():
            pick(i)

        @pl.when(i >= 1)
        def _():
            take_direct(i - 1)

        @pl.when((i >= 2) & (i - 2 < SWAP_OUT))
        def _():
            take_passed(i - 2)

    for i in range(straight - 1, SWAP_OUT):
        take_passed(i)

    @pl.loop(0, 4)
    def _(t):
        rows = pl.ds(pl.multiple_of(t * 256, 256), 256)
        g = total[rows, pl.ds(0, HID)]
        u = total[rows, pl.ds(HID, HID)]
        hidden[rows, :] = (g / (1.0 + jnp.exp(-g)) * u).astype(jnp.bfloat16)

    drain(codes.at[:, pl.ds(0, 3)], code_send)

    @pl.loop(0, straight)
    def _(i):
        drain(staged.at[i, :, pl.ds(0, 3)], stage_send.at[i])
        drain(outbound.at[i, :, pl.ds(0, 7)], send_sem.at[i])

    @pl.loop(0, SWAP_OUT)
    def _(i):
        drain(direct.at[i], pass_send.at[i])


def return_kernel(
    hidden, down, codes, out,
    combine, across, crossed, outbound, plane, sums, gathered, whole, partial, final,
    cross_send, cross_recv, send_sem, recv_sem, sum_send, sum_recv,
    part_send, part_recv, other_send, final_send, final_recv,
):
    me = Place()
    straight = outbound.shape[0]
    mine = me.x // 2

    me.greet((me.left, me.right, me.far))

    def product(t, start):
        rows = pl.ds(pl.multiple_of(t * 256, 256), 256)
        return jnp.dot(hidden[rows, :], down[0, :, columns(start)], preferred_element_type=jnp.float32)

    def cross(i):
        base = me.base(UNITS + i)

        @pl.loop(0, 4)
        def _(t):
            core, z = t // 2, lax.rem(t, 2) * 2
            for q in range(2):
                across[i, q, core, pl.ds(z, 2)] = (
                    product(t, base + q * QUARTER).astype(jnp.bfloat16).reshape(2, 4, SLOTS, PART)
                )

        for q, to in ((0, me.left), (1, me.right)):
            remote(across.at[i, q], crossed.at[i, q], cross_send.at[i], cross_recv.at[i], me.node, to)

    def send_rows(i):
        base = me.base(unit_of(i, SWAP_BACK))

        @pl.when(i < SWAP_BACK)
        def _():
            drain(crossed.at[i], cross_recv.at[i])

            @pl.loop(0, 4)
            def _(t):
                core, z = t // 2, lax.rem(t, 2) * 2
                for q in range(2):
                    other = crossed[i, q, core, pl.ds(z, 2)].reshape(256, PART).astype(jnp.float32)
                    outbound[i, q, core, pl.ds(z, 2)] = (
                        (product(t, base + q * QUARTER) + other).astype(jnp.bfloat16).reshape(2, 4, SLOTS, PART)
                    )

        @pl.when(i >= SWAP_BACK)
        def _():
            @pl.loop(0, 4)
            def _(t):
                core, z = t // 2, lax.rem(t, 2) * 2
                for q in range(2):
                    outbound[i, q, core, pl.ds(z, 2)] = (
                        product(t, base + q * QUARTER).astype(jnp.bfloat16).reshape(2, 4, SLOTS, PART)
                    )

        @pl.loop(1, 8)
        def _(step):
            index, core, node = me.across(0, step)
            remote(
                outbound.at[i, 0, core, :, index], plane.at[i, 0, me.y * 2 + me.core],
                send_sem.at[i], recv_sem.at[i], node, me.x,
            )
            index, core, node = me.across(1, step)
            remote(
                outbound.at[i, 1, core, index], plane.at[i, 1, me.z * 2 + me.core],
                send_sem.at[i], recv_sem.at[i], node, me.x,
            )

        pltpu.make_async_copy(
            outbound.at[i, 0, me.core, :, me.y], plane.at[i, 0, me.y * 2 + me.core], recv_sem.at[i]
        ).start()
        pltpu.make_async_copy(
            outbound.at[i, 1, me.core, me.z], plane.at[i, 1, me.z * 2 + me.core], recv_sem.at[i]
        ).start()

    def send_sums(i):
        drain(plane.at[i], recv_sem.at[i])
        for q in range(2):
            for s in range(4):
                both = jnp.dot(
                    combine[q, s], plane[i, q, :, s].reshape(PLANE, PART), preferred_element_type=jnp.float32
                )
                sums[i, q, s] = (both[:TOK] + both[TOK:]).astype(jnp.bfloat16)
        for step in range(1, 4):
            for q in range(2):
                index, node = me.along(q, step)
                remote(
                    sums.at[i, q, index], gathered.at[i, q, me.own(q)], sum_send.at[i], sum_recv.at[i], node, me.x
                )
        for q in range(2):
            pltpu.make_async_copy(
                sums.at[i, q, me.own(q)], gathered.at[i, q, me.own(q)], sum_recv.at[i]
            ).start()

    def send_parts(i):
        drain(gathered.at[i], sum_recv.at[i])
        for q in range(2):
            whole[i, q] = (
                (gathered[i, q, 0].astype(jnp.float32) + gathered[i, q, 1].astype(jnp.float32))
                + (gathered[i, q, 2].astype(jnp.float32) + gathered[i, q, 3].astype(jnp.float32))
            ).astype(jnp.bfloat16)

        @pl.when(i < UNITS)
        def _():
            remote(whole.at[i, 1 - mine], partial.at[i, 0], part_send.at[i], part_recv.at[i, 0], me.node, me.far)

        @pl.when(i >= UNITS)
        def _():
            unit = i - UNITS + SWAP_BACK
            for q in range(2):
                owner = 1 - me.side + 2 * q
                slot = jnp.where(owner == me.right, 1, 2)
                remote(
                    whole.at[i, q], partial.at[unit, slot],
                    other_send.at[i - UNITS], part_recv.at[unit, slot], me.node, owner,
                )

    def finish(p):
        drain(partial.at[p, 0], part_recv.at[p, 0])
        value = whole[p, mine].astype(jnp.float32) + partial[p, 0].astype(jnp.float32)
        final[p] = value.astype(jnp.bfloat16)

        @pl.when(p >= SWAP_BACK)
        def _():
            for slot in (1, 2):
                drain(partial.at[p, slot], part_recv.at[p, slot])
            value = (whole[p, mine].astype(jnp.float32) + partial[p, 0].astype(jnp.float32)) + (
                partial[p, 1].astype(jnp.float32) + partial[p, 2].astype(jnp.float32)
            )
            final[p] = value.astype(jnp.bfloat16)

        cols = columns(me.side * HALF + mine * QUARTER + p * PART)
        for to in (me.left, me.right, me.far):
            remote(final.at[p], out.at[:, cols], final_send.at[p], final_recv.at[p], me.node, to)
        out[:, cols] = final[p]

    cross(0)
    cross(1)

    for q in range(2):
        wanted = me.plane_targets(q)
        for s in range(4):
            have = codes[q, s] >> SHIFT
            unit = codes[q, s] & ((1 << SHIFT) - 1)
            sum_units = jnp.where(have[0:1] == wanted, unit[0:1], 0)
            for k in range(1, TOPK):
                sum_units += jnp.where(have[k:k + 1] == wanted, unit[k:k + 1], 0)
            low = sum_units & 7
            for h, part in enumerate((sum_units - low, low)):
                turned = jnp.transpose(part.astype(jnp.float32) * (1.0 / 1024.0))
                combine[q, s, pl.ds(h * TOK, TOK)] = turned[:TOK].astype(jnp.bfloat16)

    def piece(o):
        return lax.rem(o + SWAP_BACK, straight)

    @pl.loop(0, straight + 3)
    def _(o):
        @pl.when((o + 2 < SWAP_BACK))
        def _():
            cross(o + 2)

        @pl.when(o < straight)
        def _():
            send_rows(piece(o))

        @pl.when((o >= 1) & (o - 1 < straight))
        def _():
            send_sums(piece(o - 1))

        @pl.when((o >= 2) & (o - 2 < straight))
        def _():
            send_parts(piece(o - 2))

        @pl.when(o >= 3)
        def _():
            i = piece(o - 3)

            @pl.when(i < SWAP_BACK)
            def _():
                finish(i)

            @pl.when(i >= UNITS)
            def _():
                finish(i - UNITS + SWAP_BACK)

    @pl.loop(0, straight)
    def _(i):
        drain(plane.at[i, :, pl.ds(0, 7)], send_sem.at[i])
        drain(gathered.at[i, :, pl.ds(0, 3)], sum_send.at[i])

    @pl.loop(0, SWAP_BACK)
    def _(i):
        drain(across.at[i], cross_send.at[i])

    @pl.loop(0, UNITS)
    def _(p):
        drain(whole.at[p, 0], part_send.at[p])
        drain(partial.at[p], final_send.at[p])
        drain(partial.at[p], final_recv.at[p])

    @pl.loop(0, UNITS - SWAP_BACK)
    def _(i):
        drain(whole.at[i], other_send.at[i])


def local(tokens, routes, route_weight, expert_gate, expert_up, expert_down):
    flat = routes.reshape(-1)
    labels = jnp.arange(EXPERTS, dtype=jnp.int32)
    onehot = (flat[:, None] == labels[None, :]).astype(jnp.int32)
    before = jnp.cumsum(onehot, axis=0) - onehot
    slot = jnp.sum(before * onehot, axis=1)
    target = (flat * SLOTS + slot).reshape(TOK, TOPK)
    code = jnp.pad(
        ((target << SHIFT) | route_weight).T, ((0, 0), (0, LANES - TOK)), constant_values=ROWS << SHIFT
    )

    vmem = pl.BlockSpec(memory_space=pltpu.VMEM)
    anywhere = pl.BlockSpec(memory_space=pl.ANY)
    dma = pltpu.SemaphoreType.DMA
    bf16 = jnp.bfloat16
    out_count, back_count = 2 * UNITS - SWAP_OUT, 2 * UNITS - SWAP_BACK
    by_source = (2, 2, 4, 4, SLOTS, PART)
    by_plane = (2, 8, 4, SLOTS, PART)
    hidden, codes = pl.pallas_call(
        dispatch_kernel,
        out_shape=(
            jax.ShapeDtypeStruct((ROWS, HID), bf16),
            jax.ShapeDtypeStruct((2, 4, TOPK, LANES), jnp.int32),
        ),
        in_specs=[vmem, vmem, anywhere, anywhere],
        out_specs=(vmem, vmem),
        scratch_shapes=[
            pltpu.VMEM((2, 4, TOPK, LANES), jnp.int32),
            pltpu.VMEM((2, 4, PLANE, LANES), bf16),
            pltpu.VMEM((out_count, 2, 4, TOK, PART), bf16),
            pltpu.VMEM((out_count,) + by_plane, bf16),
            pltpu.VMEM((out_count,) + by_source, bf16),
            pltpu.VMEM((SWAP_OUT,) + by_source, bf16),
            pltpu.VMEM((2 * UNITS, 2 * PART, 2 * HID), bf16),
            pltpu.VMEM((ROWS, 2 * HID), jnp.float32),
            dma(()), dma(()),
            dma((out_count,)), dma((out_count,)), dma((out_count,)), dma((out_count,)),
            dma((SWAP_OUT,)), dma((SWAP_OUT,)), dma((2 * UNITS,)),
        ],
        compiler_params=pltpu.CompilerParams(
            collective_id=0, has_side_effects=True, vmem_limit_bytes=56 * MIB
        ),
        name="dispatch",
    )(code, tokens, expert_gate, expert_up)
    return pl.pallas_call(
        return_kernel,
        out_shape=jax.ShapeDtypeStruct((TOK, D), bf16),
        in_specs=[vmem, vmem, vmem],
        out_specs=vmem,
        scratch_shapes=[
            pltpu.VMEM((2, 4, 2 * TOK, PLANE), bf16),
            pltpu.VMEM((SWAP_BACK,) + by_source, bf16),
            pltpu.VMEM((SWAP_BACK,) + by_source, bf16),
            pltpu.VMEM((back_count,) + by_source, bf16),
            pltpu.VMEM((back_count,) + by_plane, bf16),
            pltpu.VMEM((back_count, 2, 4, TOK, PART), bf16),
            pltpu.VMEM((back_count, 2, 4, TOK, PART), bf16),
            pltpu.VMEM((back_count, 2, TOK, PART), bf16),
            pltpu.VMEM((UNITS, 3, TOK, PART), bf16),
            pltpu.VMEM((UNITS, TOK, PART), bf16),
            dma((SWAP_BACK,)), dma((SWAP_BACK,)),
            dma((back_count,)), dma((back_count,)), dma((back_count,)), dma((back_count,)),
            dma((UNITS,)), dma((UNITS, 3)), dma((UNITS - SWAP_BACK,)), dma((UNITS,)), dma((UNITS,)),
        ],
        compiler_params=pltpu.CompilerParams(
            collective_id=1, has_side_effects=True, vmem_limit_bytes=56 * MIB
        ),
        name="give_back",
    )(hidden, expert_down, codes)


def solution(mesh):
    return jax.shard_map(
        local,
        mesh=mesh,
        in_specs=(
            P("node", None),
            P("node", None),
            P("node", None),
            P("node", None, "local"),
            P("node", None, "local"),
            P("node", "local", None),
        ),
        out_specs=P("node", None),
        check_vma=False,
    )
```

```python
import jax
import jax.numpy as jnp
from jax import lax
from jax.experimental import pallas as pl
from jax.experimental.pallas import tpu as pltpu
from jax.sharding import PartitionSpec as P

EXPERTS = 32
SLOTS = 32
ROWS = 32 * SLOTS
D = 7168
HALF = D // 2
QUARTER = D // 4
HID = 512
TOK = 96
TOPK = 8
LANES = 128
UNITS = 7
PART = QUARTER // UNITS
SWAP_OUT = 5
SWAP_BACK = 4
PLANE = 8 * SLOTS
SHIFT = 11
STAGE_LEAD = 2
PICK_LEAD = 1
PASS_LAG = 5
HOPS = (1, 3, 2)
PLACES = ((1, 0), (3, 0), (2, 0), (1, 1), (3, 1), (2, 1), (0, 1))
MESH = pl.DeviceIdType.MESH
MIB = 1 << 20


def columns(start):
    return pl.ds(pl.multiple_of(start, PART), PART)


def drain(ref, sem):
    pltpu.make_async_copy(ref, ref, sem).wait()


def remote(src, dst, send_sem, recv_sem, node, x):
    pltpu.make_async_remote_copy(
        src_ref=src, dst_ref=dst, send_sem=send_sem, recv_sem=recv_sem,
        device_id=(node, x), device_id_type=MESH,
    ).start()


class Place:
    def __init__(self):
        self.node, self.x = lax.axis_index("node"), lax.axis_index("local")
        self.core = lax.rem(self.node, 2)
        self.y = lax.rem(self.node // 2, 4)
        self.z = self.node // 8
        self.right, self.left = lax.rem(self.x + 1, 4), lax.rem(self.x + 3, 4)
        self.far = lax.rem(self.x + 2, 4)
        self.side = lax.rem(self.x, 2)

    def at(self, z, y, core):
        return (z * 4 + y) * 2 + core

    def turn(self, hops):
        return jnp.where(self.core == 0, hops, (4 - hops) % 4)

    def along(self, q, hops):
        if q == 0:
            index = lax.rem(self.z + self.turn(hops), 4)
            return index, self.at(index, self.y, self.core)
        index = lax.rem(self.y + self.turn(hops), 4)
        return index, self.at(self.z, index, self.core)

    def across(self, q, hops, other):
        core = self.core if other == 0 else 1 - self.core
        if q == 0:
            index = lax.rem(self.y + self.turn(hops), 4)
            return index, core, self.at(self.z, index, core)
        index = lax.rem(self.z + self.turn(hops), 4)
        return index, core, self.at(index, self.y, core)

    def own(self, q):
        return self.z if q == 0 else self.y

    def base(self, j):
        return jnp.where(j < UNITS, self.side * HALF + j * PART, (1 - self.side) * HALF + (j - UNITS) * PART)

    def plane_experts(self, q):
        row = lax.broadcasted_iota(jnp.int32, (PLANE, LANES), 0)
        if q == 0:
            return (row >> 5) + self.z * 8, row & (SLOTS - 1)
        return (row >> 6) * 8 + self.y * 2 + ((row >> 5) & 1), row & (SLOTS - 1)

    def greet(self, others):
        barrier = pltpu.get_barrier_semaphore()

        def hello(node, x):
            pl.semaphore_signal(barrier, inc=1, device_id=(node, x), device_id_type=MESH)

        for hops, other in PLACES:
            hello(self.across(0, hops, other)[2], self.x)
            if hops:
                hello(self.across(1, hops, other)[2], self.x)
        for other in others:
            hello(self.node, other)
        pl.semaphore_wait(barrier, 13 + len(others))


def unit_of(i, swapped):
    return jnp.where(i < UNITS, i, i + swapped)


def dispatch_kernel(
    code, tokens, gate, up, hidden, combine,
    codes, select, staged, outbound, direct, passed, weights, total,
    code_send, code_recv, stage_send, stage_recv, send_sem, recv_sem, pass_send, pass_recv, weight_sem,
):
    me = Place()
    straight = direct.shape[0]

    me.greet((me.left, me.right))

    def stage(i):
        base = me.base(unit_of(i, SWAP_OUT))
        for hops in HOPS:
            for q in range(2):
                remote(
                    tokens.at[:, columns(base + q * QUARTER)], staged.at[i, q, me.own(q)],
                    stage_send.at[i], stage_recv.at[i], me.along(q, hops)[1], me.x,
                )
        for q in range(2):
            pltpu.make_async_copy(
                tokens.at[:, columns(base + q * QUARTER)], staged.at[i, q, me.own(q)], stage_recv.at[i]
            ).start()

    for q in range(2):
        for hops in HOPS:
            remote(code, codes.at[q, me.own(q)], code_send, code_recv, me.along(q, hops)[1], me.x)
        pltpu.make_async_copy(code, codes.at[q, me.own(q)], code_recv).start()
    for i in range(STAGE_LEAD):
        stage(i)

    @pl.loop(0, 2 * UNITS)
    def _(j):
        for q in range(2):
            for m, source in enumerate((gate, up)):
                pltpu.make_async_copy(
                    source.at[0, columns(me.base(j) + q * QUARTER)],
                    weights.at[j, pl.ds(q * PART, PART), pl.ds(m * HID, HID)],
                    weight_sem.at[j],
                ).start()

    drain(codes, code_recv)
    lane = lax.broadcasted_iota(jnp.int32, (LANES, LANES), 1)
    earlier = (lax.broadcasted_iota(jnp.int32, (LANES, LANES), 0) < lane).astype(jnp.float32).astype(jnp.bfloat16)
    for q in range(2):
        expert, slot = me.plane_experts(q)
        for s in range(4):
            chosen = codes[q, s] >> SHIFT
            hit = chosen[0:1] == expert
            for k in range(1, TOPK):
                hit = hit | (chosen[k:k + 1] == expert)
            before = jnp.dot(
                hit.astype(jnp.float32).astype(jnp.bfloat16), earlier, preferred_element_type=jnp.float32
            )
            hit = hit & (before == slot.astype(jnp.float32))
            select[q, s] = hit.astype(jnp.float32).astype(jnp.bfloat16)

    def weigh():
        for q in range(2):
            expert, slot = me.plane_experts(q)
            for s in range(4):
                chosen = codes[q, s] >> SHIFT
                weight = codes[q, s] & ((1 << SHIFT) - 1)
                unit = jnp.where(chosen[0:1] == expert, weight[0:1], 0)
                for k in range(1, TOPK):
                    unit += jnp.where(chosen[k:k + 1] == expert, weight[k:k + 1], 0)
                unit = jnp.where(select[q, s].astype(jnp.float32) > 0.5, unit, 0)
                low = unit & 7
                for h, part in enumerate((unit - low, low)):
                    turned = jnp.transpose(part.astype(jnp.float32) * (1.0 / 1024.0))
                    combine[q, s, pl.ds(h * TOK, TOK)] = turned[:TOK].astype(jnp.bfloat16)

    def pick(i):
        drain(staged.at[i], stage_recv.at[i])
        for q in range(2):
            for s in range(4):
                outbound[i, q, :, s] = jnp.dot(
                    select[q, s, :, :TOK], staged[i, q, s], preferred_element_type=jnp.float32
                ).astype(jnp.bfloat16).reshape(8, SLOTS, PART)

        for hops, other in PLACES:
            index, core, node = me.across(0, hops, other)
            remote(
                outbound.at[i, 0, index * 2 + core], direct.at[i, 0, me.core, :, me.y],
                send_sem.at[i], recv_sem.at[i], node, me.x,
            )
            index, core, node = me.across(1, hops, other)
            remote(
                outbound.at[i, 1, index * 2 + core], direct.at[i, 1, me.core, me.z],
                send_sem.at[i], recv_sem.at[i], node, me.x,
            )

        pltpu.make_async_copy(
            outbound.at[i, 0, me.y * 2 + me.core], direct.at[i, 0, me.core, :, me.y], recv_sem.at[i]
        ).start()
        pltpu.make_async_copy(
            outbound.at[i, 1, me.z * 2 + me.core], direct.at[i, 1, me.core, me.z], recv_sem.at[i]
        ).start()

    def add_product(rows_ref, i, j, first=False):
        drain(weights.at[j], weight_sem.at[j])

        @pl.loop(0, 4)
        def _(t):
            core, z = t // 2, lax.rem(t, 2) * 2
            rows = pl.ds(pl.multiple_of(t * 256, 256), 256)
            left = jnp.concatenate(
                [rows_ref[i, q, core, pl.ds(z, 2)].reshape(256, PART) for q in range(2)], axis=1
            )
            for m in range(2):
                cols = pl.ds(m * HID, HID)
                value = jnp.dot(left, weights[j, :, cols], preferred_element_type=jnp.float32)
                total[rows, cols] = value if first else total[rows, cols] + value

    def take_direct(i):
        drain(direct.at[i], recv_sem.at[i])

        @pl.when(i < SWAP_OUT)
        def _():
            for q, to in ((0, me.right), (1, me.left)):
                remote(direct.at[i, q], passed.at[i, q], pass_send.at[i], pass_recv.at[i], me.node, to)

        @pl.when(i == 0)
        def _():
            add_product(direct, i, unit_of(i, SWAP_OUT), first=True)

        @pl.when(i > 0)
        def _():
            add_product(direct, i, unit_of(i, SWAP_OUT))

    def take_passed(i):
        drain(passed.at[i], pass_recv.at[i])
        add_product(passed, i, UNITS + i)

    steps = max(straight + PICK_LEAD, SWAP_OUT + PASS_LAG)

    @pl.loop(0, steps)
    def _(i):
        @pl.when(i + STAGE_LEAD < straight)
        def _():
            stage(i + STAGE_LEAD)

        @pl.when(i < straight)
        def _():
            pick(i)

        @pl.when(i == 2)
        def _():
            weigh()

        @pl.when((i >= PICK_LEAD) & (i - PICK_LEAD < straight))
        def _():
            take_direct(i - PICK_LEAD)

        @pl.when((i >= PASS_LAG) & (i - PASS_LAG < SWAP_OUT))
        def _():
            take_passed(i - PASS_LAG)

    @pl.loop(0, 4)
    def _(t):
        rows = pl.ds(pl.multiple_of(t * 256, 256), 256)
        g = total[rows, pl.ds(0, HID)]
        u = total[rows, pl.ds(HID, HID)]
        hidden[rows, :] = (g / (1.0 + jnp.exp(-g)) * u).astype(jnp.bfloat16)

    drain(codes.at[:, pl.ds(0, 3)], code_send)

    @pl.loop(0, straight)
    def _(i):
        drain(staged.at[i, :, pl.ds(0, 3)], stage_send.at[i])
        drain(outbound.at[i, :, pl.ds(0, 7)], send_sem.at[i])

    @pl.loop(0, SWAP_OUT)
    def _(i):
        drain(direct.at[i], pass_send.at[i])


def return_kernel(
    hidden, down_hbm, combine, out,
    down, across, crossed, outbound, plane, sums, gathered, whole, partial, final,
    cross_send, cross_recv, send_sem, recv_sem, sum_send, sum_recv,
    part_send, part_recv, other_send, final_send, final_recv, down_sem,
):
    me = Place()
    straight = outbound.shape[0]
    mine = me.x // 2

    pltpu.make_async_copy(down_hbm, down, down_sem).start()
    me.greet((me.left, me.right, me.far))
    drain(down, down_sem)

    def product(t, base):
        rows = pl.ds(pl.multiple_of(t * 256, 256), 256)
        right = jnp.concatenate([down[0, :, columns(base + q * QUARTER)] for q in range(2)], axis=1)
        both = jnp.dot(hidden[rows, :], right, preferred_element_type=jnp.float32)
        return both[:, :PART], both[:, PART:]

    def cross(i):
        base = me.base(UNITS + i)

        @pl.loop(0, 4)
        def _(t):
            core, z = t // 2, lax.rem(t, 2) * 2
            for q, own in enumerate(product(t, base)):
                across[i, q, core, pl.ds(z, 2)] = own.astype(jnp.bfloat16).reshape(2, 4, SLOTS, PART)

        for q, to in ((0, me.left), (1, me.right)):
            remote(across.at[i, q], crossed.at[i, q], cross_send.at[i], cross_recv.at[i], me.node, to)

    def send_rows(i):
        base = me.base(unit_of(i, SWAP_BACK))

        @pl.when(i < SWAP_BACK)
        def _():
            drain(crossed.at[i], cross_recv.at[i])

            @pl.loop(0, 4)
            def _(t):
                core, z = t // 2, lax.rem(t, 2) * 2
                for q, own in enumerate(product(t, base)):
                    other = crossed[i, q, core, pl.ds(z, 2)].reshape(256, PART).astype(jnp.float32)
                    outbound[i, q, core, pl.ds(z, 2)] = (
                        (own + other).astype(jnp.bfloat16).reshape(2, 4, SLOTS, PART)
                    )

        @pl.when(i >= SWAP_BACK)
        def _():
            @pl.loop(0, 4)
            def _(t):
                core, z = t // 2, lax.rem(t, 2) * 2
                for q, own in enumerate(product(t, base)):
                    outbound[i, q, core, pl.ds(z, 2)] = own.astype(jnp.bfloat16).reshape(2, 4, SLOTS, PART)

        for hops, other in PLACES:
            index, core, node = me.across(0, hops, other)
            remote(
                outbound.at[i, 0, core, :, index], plane.at[i, 0, me.y * 2 + me.core],
                send_sem.at[i], recv_sem.at[i], node, me.x,
            )
            index, core, node = me.across(1, hops, other)
            remote(
                outbound.at[i, 1, core, index], plane.at[i, 1, me.z * 2 + me.core],
                send_sem.at[i], recv_sem.at[i], node, me.x,
            )

        pltpu.make_async_copy(
            outbound.at[i, 0, me.core, :, me.y], plane.at[i, 0, me.y * 2 + me.core], recv_sem.at[i]
        ).start()
        pltpu.make_async_copy(
            outbound.at[i, 1, me.core, me.z], plane.at[i, 1, me.z * 2 + me.core], recv_sem.at[i]
        ).start()

    def send_sums(i):
        drain(plane.at[i], recv_sem.at[i])
        for q in range(2):
            for s in range(4):
                both = jnp.dot(
                    combine[q, s], plane[i, q, :, s].reshape(PLANE, PART), preferred_element_type=jnp.float32
                )
                sums[i, q, s] = (both[:TOK] + both[TOK:]).astype(jnp.bfloat16)
        for hops in HOPS:
            for q in range(2):
                index, node = me.along(q, hops)
                remote(
                    sums.at[i, q, index], gathered.at[i, q, me.own(q)], sum_send.at[i], sum_recv.at[i], node, me.x
                )
        for q in range(2):
            pltpu.make_async_copy(
                sums.at[i, q, me.own(q)], gathered.at[i, q, me.own(q)], sum_recv.at[i]
            ).start()

    def send_parts(i):
        drain(gathered.at[i], sum_recv.at[i])
        for q in range(2):
            whole[i, q] = (
                (gathered[i, q, 0].astype(jnp.float32) + gathered[i, q, 1].astype(jnp.float32))
                + (gathered[i, q, 2].astype(jnp.float32) + gathered[i, q, 3].astype(jnp.float32))
            ).astype(jnp.bfloat16)

        @pl.when(i < UNITS)
        def _():
            remote(whole.at[i, 1 - mine], partial.at[i, 0], part_send.at[i], part_recv.at[i, 0], me.node, me.far)

        @pl.when(i >= UNITS)
        def _():
            unit = i - UNITS + SWAP_BACK
            for q in range(2):
                owner = 1 - me.side + 2 * q
                slot = jnp.where(owner == me.right, 1, 2)
                remote(
                    whole.at[i, q], partial.at[unit, slot],
                    other_send.at[i - UNITS], part_recv.at[unit, slot], me.node, owner,
                )

    def finish(p):
        drain(partial.at[p, 0], part_recv.at[p, 0])
        value = whole[p, mine].astype(jnp.float32) + partial[p, 0].astype(jnp.float32)
        final[p] = value.astype(jnp.bfloat16)

        @pl.when(p >= SWAP_BACK)
        def _():
            for slot in (1, 2):
                drain(partial.at[p, slot], part_recv.at[p, slot])
            value = (whole[p, mine].astype(jnp.float32) + partial[p, 0].astype(jnp.float32)) + (
                partial[p, 1].astype(jnp.float32) + partial[p, 2].astype(jnp.float32)
            )
            final[p] = value.astype(jnp.bfloat16)

        cols = columns(me.side * HALF + mine * QUARTER + p * PART)
        for to in (me.left, me.right, me.far):
            remote(final.at[p], out.at[:, cols], final_send.at[p], final_recv.at[p], me.node, to)
        out[:, cols] = final[p]

    def piece(o):
        return lax.rem(o + SWAP_BACK, straight)

    @pl.loop(0, straight + 3)
    def _(o):
        @pl.when(o < straight)
        def _():
            send_rows(piece(o))

        @pl.when(o < SWAP_BACK)
        def _():
            cross(o)

        @pl.when((o >= 1) & (o - 1 < straight))
        def _():
            send_sums(piece(o - 1))

        @pl.when((o >= 2) & (o - 2 < straight))
        def _():
            send_parts(piece(o - 2))

        @pl.when(o >= 3)
        def _():
            i = piece(o - 3)

            @pl.when(i < SWAP_BACK)
            def _():
                finish(i)

            @pl.when(i >= UNITS)
            def _():
                finish(i - UNITS + SWAP_BACK)

    @pl.loop(0, straight)
    def _(i):
        drain(plane.at[i, :, pl.ds(0, 7)], send_sem.at[i])
        drain(gathered.at[i, :, pl.ds(0, 3)], sum_send.at[i])

    @pl.loop(0, SWAP_BACK)
    def _(i):
        drain(across.at[i], cross_send.at[i])

    @pl.loop(0, UNITS)
    def _(p):
        drain(whole.at[p, 0], part_send.at[p])
        drain(partial.at[p], final_send.at[p])
        drain(partial.at[p], final_recv.at[p])

    @pl.loop(0, UNITS - SWAP_BACK)
    def _(i):
        drain(whole.at[i], other_send.at[i])


def local(tokens, routes, route_weight, expert_gate, expert_up, expert_down):
    code = jnp.pad(
        ((routes << SHIFT) | route_weight).T, ((0, 0), (0, LANES - TOK)), constant_values=EXPERTS << SHIFT
    )

    vmem = pl.BlockSpec(memory_space=pltpu.VMEM)
    anywhere = pl.BlockSpec(memory_space=pl.ANY)
    dma = pltpu.SemaphoreType.DMA
    bf16 = jnp.bfloat16
    out_count, back_count = 2 * UNITS - SWAP_OUT, 2 * UNITS - SWAP_BACK
    by_source = (2, 2, 4, 4, SLOTS, PART)
    by_plane = (2, 8, 4, SLOTS, PART)
    hidden, combine = pl.pallas_call(
        dispatch_kernel,
        out_shape=(
            jax.ShapeDtypeStruct((ROWS, HID), bf16),
            jax.ShapeDtypeStruct((2, 4, 2 * TOK, PLANE), bf16),
        ),
        in_specs=[vmem, vmem, anywhere, anywhere],
        out_specs=(vmem, vmem),
        scratch_shapes=[
            pltpu.VMEM((2, 4, TOPK, LANES), jnp.int32),
            pltpu.VMEM((2, 4, PLANE, LANES), bf16),
            pltpu.VMEM((out_count, 2, 4, TOK, PART), bf16),
            pltpu.VMEM((out_count,) + by_plane, bf16),
            pltpu.VMEM((out_count,) + by_source, bf16),
            pltpu.VMEM((SWAP_OUT,) + by_source, bf16),
            pltpu.VMEM((2 * UNITS, 2 * PART, 2 * HID), bf16),
            pltpu.VMEM((ROWS, 2 * HID), jnp.float32),
            dma(()), dma(()),
            dma((out_count,)), dma((out_count,)), dma((out_count,)), dma((out_count,)),
            dma((SWAP_OUT,)), dma((SWAP_OUT,)), dma((2 * UNITS,)),
        ],
        compiler_params=pltpu.CompilerParams(
            collective_id=0, has_side_effects=True, vmem_limit_bytes=56 * MIB
        ),
        name="dispatch",
    )(code, tokens, expert_gate, expert_up)
    return pl.pallas_call(
        return_kernel,
        out_shape=jax.ShapeDtypeStruct((TOK, D), bf16),
        in_specs=[vmem, anywhere, vmem],
        out_specs=vmem,
        scratch_shapes=[
            pltpu.VMEM((1, HID, D), bf16),
            pltpu.VMEM((SWAP_BACK,) + by_source, bf16),
            pltpu.VMEM((SWAP_BACK,) + by_source, bf16),
            pltpu.VMEM((back_count,) + by_source, bf16),
            pltpu.VMEM((back_count,) + by_plane, bf16),
            pltpu.VMEM((back_count, 2, 4, TOK, PART), bf16),
            pltpu.VMEM((back_count, 2, 4, TOK, PART), bf16),
            pltpu.VMEM((back_count, 2, TOK, PART), bf16),
            pltpu.VMEM((UNITS, 3, TOK, PART), bf16),
            pltpu.VMEM((UNITS, TOK, PART), bf16),
            dma((SWAP_BACK,)), dma((SWAP_BACK,)),
            dma((back_count,)), dma((back_count,)), dma((back_count,)), dma((back_count,)),
            dma((UNITS,)), dma((UNITS, 3)), dma((UNITS - SWAP_BACK,)), dma((UNITS,)), dma((UNITS,)), dma(()),
        ],
        compiler_params=pltpu.CompilerParams(
            collective_id=1, has_side_effects=True, vmem_limit_bytes=56 * MIB
        ),
        name="give_back",
    )(hidden, expert_down, combine)


def solution(mesh):
    return jax.shard_map(
        local,
        mesh=mesh,
        in_specs=(
            P("node", None),
            P("node", None),
            P("node", None),
            P("node", None, "local"),
            P("node", None, "local"),
            P("node", "local", None),
        ),
        out_specs=P("node", None),
        check_vma=False,
    )
```

```python
import jax
import jax.numpy as jnp
from jax import lax
from jax.experimental import pallas as pl
from jax.experimental.pallas import tpu as pltpu
from jax.sharding import PartitionSpec as P

EXPERTS = 32
SLOTS = 32
ROWS = 32 * SLOTS
D = 7168
HALF = D // 2
QUARTER = D // 4
HID = 512
TOK = 96
TOPK = 8
LANES = 128
UNITS_OUT = 14
UNITS_BACK = 7
PART_OUT = QUARTER // UNITS_OUT
PART_BACK = QUARTER // UNITS_BACK
SWAP_OUT = 10
SWAP_BACK = 5
PLANE = 8 * SLOTS
SHIFT = 11
STAGE_LEAD = 3
PICK_LEAD = 2
ROW_LEAD = 2
LATE = 0
PASS_LAG = 9
HOPS = (1, 3, 2)
PLACES = ((1, 0), (3, 0), (2, 0), (1, 1), (3, 1), (2, 1), (0, 1))
MESH = pl.DeviceIdType.MESH
MIB = 1 << 20


def columns(start, size):
    return pl.ds(pl.multiple_of(start, size), size)


def drain(ref, sem):
    pltpu.make_async_copy(ref, ref, sem).wait()


def remote(src, dst, send_sem, recv_sem, node, x):
    pltpu.make_async_remote_copy(
        src_ref=src, dst_ref=dst, send_sem=send_sem, recv_sem=recv_sem,
        device_id=(node, x), device_id_type=MESH,
    ).start()


class Place:
    def __init__(self, units):
        self.units = units
        self.node, self.x = lax.axis_index("node"), lax.axis_index("local")
        self.core = lax.rem(self.node, 2)
        self.y = lax.rem(self.node // 2, 4)
        self.z = self.node // 8
        self.right, self.left = lax.rem(self.x + 1, 4), lax.rem(self.x + 3, 4)
        self.far = lax.rem(self.x + 2, 4)
        self.side = lax.rem(self.x, 2)

    def at(self, z, y, core):
        return (z * 4 + y) * 2 + core

    def turn(self, hops):
        return jnp.where(self.core == 0, hops, (4 - hops) % 4)

    def along(self, q, hops):
        if q == 0:
            index = lax.rem(self.z + self.turn(hops), 4)
            return index, self.at(index, self.y, self.core)
        index = lax.rem(self.y + self.turn(hops), 4)
        return index, self.at(self.z, index, self.core)

    def across(self, q, hops, other):
        core = self.core if other == 0 else 1 - self.core
        if q == 0:
            index = lax.rem(self.y + self.turn(hops), 4)
            return index, core, self.at(self.z, index, core)
        index = lax.rem(self.z + self.turn(hops), 4)
        return index, core, self.at(index, self.y, core)

    def own(self, q):
        return self.z if q == 0 else self.y

    def base(self, j):
        half = jnp.where(j < self.units, self.side, 1 - self.side)
        return half * HALF + lax.rem(j, self.units) * (QUARTER // self.units)

    def plane_experts(self, q):
        row = lax.broadcasted_iota(jnp.int32, (PLANE, LANES), 0)
        if q == 0:
            return (row >> 5) + self.z * 8, row & (SLOTS - 1)
        return (row >> 6) * 8 + self.y * 2 + ((row >> 5) & 1), row & (SLOTS - 1)

    def greet(self, others):
        barrier = pltpu.get_barrier_semaphore()

        def hello(node, x):
            pl.semaphore_signal(barrier, inc=1, device_id=(node, x), device_id_type=MESH)

        for hops, other in PLACES:
            hello(self.across(0, hops, other)[2], self.x)
            if hops:
                hello(self.across(1, hops, other)[2], self.x)
        for other in others:
            hello(self.node, other)
        pl.semaphore_wait(barrier, 13 + len(others))

    def unit_of(self, i, swapped):
        return jnp.where(i < self.units, i, i + swapped)


def dispatch_kernel(
    code, tokens, gate, up, hidden, combine,
    codes, select, staged, outbound, direct, passed, weights, total,
    code_send, code_recv, stage_send, stage_recv, send_sem, recv_sem, pass_send, pass_recv, weight_sem,
):
    me = Place(UNITS_OUT)
    straight = direct.shape[0]

    me.greet((me.left, me.right))

    def stage(i):
        base = me.base(me.unit_of(i, SWAP_OUT))
        for hops in HOPS:
            for q in range(2):
                remote(
                    tokens.at[:, columns(base + q * QUARTER, PART_OUT)], staged.at[i, q, me.own(q)],
                    stage_send.at[i], stage_recv.at[i], me.along(q, hops)[1], me.x,
                )
        for q in range(2):
            pltpu.make_async_copy(
                tokens.at[:, columns(base + q * QUARTER, PART_OUT)], staged.at[i, q, me.own(q)], stage_recv.at[i]
            ).start()

    for q in range(2):
        for hops in HOPS:
            remote(code, codes.at[q, me.own(q)], code_send, code_recv, me.along(q, hops)[1], me.x)
        pltpu.make_async_copy(code, codes.at[q, me.own(q)], code_recv).start()
    for i in range(STAGE_LEAD):
        stage(i)

    @pl.loop(0, 2 * UNITS_OUT)
    def _(j):
        for q in range(2):
            for m, source in enumerate((gate, up)):
                pltpu.make_async_copy(
                    source.at[0, columns(me.base(j) + q * QUARTER, PART_OUT)],
                    weights.at[j, pl.ds(q * PART_OUT, PART_OUT), pl.ds(m * HID, HID)],
                    weight_sem.at[j],
                ).start()

    drain(codes, code_recv)
    lane = lax.broadcasted_iota(jnp.int32, (LANES, LANES), 1)
    earlier = (lax.broadcasted_iota(jnp.int32, (LANES, LANES), 0) < lane).astype(jnp.float32).astype(jnp.bfloat16)
    for q in range(2):
        expert, slot = me.plane_experts(q)
        for s in range(4):
            chosen = codes[q, s] >> SHIFT
            hit = chosen[0:1] == expert
            for k in range(1, TOPK):
                hit = hit | (chosen[k:k + 1] == expert)
            before = jnp.dot(
                hit.astype(jnp.float32).astype(jnp.bfloat16), earlier, preferred_element_type=jnp.float32
            )
            hit = hit & (before == slot.astype(jnp.float32))
            select[q, s] = hit.astype(jnp.float32).astype(jnp.bfloat16)

    def weigh():
        for q in range(2):
            expert, slot = me.plane_experts(q)
            for s in range(4):
                chosen = codes[q, s] >> SHIFT
                weight = codes[q, s] & ((1 << SHIFT) - 1)
                unit = jnp.where(chosen[0:1] == expert, weight[0:1], 0)
                for k in range(1, TOPK):
                    unit += jnp.where(chosen[k:k + 1] == expert, weight[k:k + 1], 0)
                unit = jnp.where(select[q, s].astype(jnp.float32) > 0.5, unit, 0)
                low = unit & 7
                for h, part in enumerate((unit - low, low)):
                    turned = jnp.transpose(part.astype(jnp.float32) * (1.0 / 1024.0))
                    combine[q, s, pl.ds(h * TOK, TOK)] = turned[:TOK].astype(jnp.bfloat16)

    def pick(i):
        drain(staged.at[i], stage_recv.at[i])
        for q in range(2):
            for s in range(4):
                outbound[i, q, :, s] = jnp.dot(
                    select[q, s, :, :TOK], staged[i, q, s], preferred_element_type=jnp.float32
                ).astype(jnp.bfloat16).reshape(8, SLOTS, PART_OUT)

        for hops, other in PLACES:
            index, core, node = me.across(0, hops, other)
            remote(
                outbound.at[i, 0, index * 2 + core], direct.at[i, 0, me.core, :, me.y],
                send_sem.at[i], recv_sem.at[i], node, me.x,
            )
            index, core, node = me.across(1, hops, other)
            remote(
                outbound.at[i, 1, index * 2 + core], direct.at[i, 1, me.core, me.z],
                send_sem.at[i], recv_sem.at[i], node, me.x,
            )

        pltpu.make_async_copy(
            outbound.at[i, 0, me.y * 2 + me.core], direct.at[i, 0, me.core, :, me.y], recv_sem.at[i]
        ).start()
        pltpu.make_async_copy(
            outbound.at[i, 1, me.z * 2 + me.core], direct.at[i, 1, me.core, me.z], recv_sem.at[i]
        ).start()

    def add_product(rows_ref, i, j, first=False):
        drain(weights.at[j], weight_sem.at[j])

        @pl.loop(0, 4)
        def _(t):
            core, z = t // 2, lax.rem(t, 2) * 2
            rows = pl.ds(pl.multiple_of(t * 256, 256), 256)
            left = jnp.concatenate(
                [rows_ref[i, q, core, pl.ds(z, 2)].reshape(256, PART_OUT) for q in range(2)], axis=1
            )
            for m in range(2):
                cols = pl.ds(m * HID, HID)
                value = jnp.dot(left, weights[j, :, cols], preferred_element_type=jnp.float32)
                total[rows, cols] = value if first else total[rows, cols] + value

    def take_direct(i):
        drain(direct.at[i], recv_sem.at[i])

        @pl.when(i < SWAP_OUT)
        def _():
            for q, to in ((0, me.right), (1, me.left)):
                remote(direct.at[i, q], passed.at[i, q], pass_send.at[i], pass_recv.at[i], me.node, to)

        @pl.when(i == 0)
        def _():
            add_product(direct, i, me.unit_of(i, SWAP_OUT), first=True)

        @pl.when(i > 0)
        def _():
            add_product(direct, i, me.unit_of(i, SWAP_OUT))

    def take_passed(i):
        drain(passed.at[i], pass_recv.at[i])
        add_product(passed, i, UNITS_OUT + i)

    steps = max(straight + PICK_LEAD, SWAP_OUT + PASS_LAG)

    @pl.loop(0, steps)
    def _(i):
        @pl.when(i + STAGE_LEAD < straight)
        def _():
            stage(i + STAGE_LEAD)

        @pl.when(i < straight)
        def _():
            pick(i)

        @pl.when(i == 2)
        def _():
            weigh()

        @pl.when((i >= PICK_LEAD) & (i - PICK_LEAD < straight))
        def _():
            take_direct(i - PICK_LEAD)

        @pl.when((i >= PASS_LAG) & (i - PASS_LAG < SWAP_OUT))
        def _():
            take_passed(i - PASS_LAG)

    @pl.loop(0, 4)
    def _(t):
        rows = pl.ds(pl.multiple_of(t * 256, 256), 256)
        g = total[rows, pl.ds(0, HID)]
        u = total[rows, pl.ds(HID, HID)]
        hidden[rows, :] = (g / (1.0 + jnp.exp(-g)) * u).astype(jnp.bfloat16)

    drain(codes.at[:, pl.ds(0, 3)], code_send)

    @pl.loop(0, straight)
    def _(i):
        drain(staged.at[i, :, pl.ds(0, 3)], stage_send.at[i])
        drain(outbound.at[i, :, pl.ds(0, 7)], send_sem.at[i])

    @pl.loop(0, SWAP_OUT)
    def _(i):
        drain(direct.at[i], pass_send.at[i])


def return_kernel(
    hidden, down_hbm, combine, out,
    down, across, crossed, outbound, plane, sums, gathered, whole, partial, final,
    cross_send, cross_recv, send_sem, recv_sem, sum_send, sum_recv,
    part_send, part_recv, other_send, final_send, final_recv, down_sem,
):
    me = Place(UNITS_BACK)
    straight = outbound.shape[0]
    mine = me.x // 2

    pltpu.make_async_copy(down_hbm, down, down_sem).start()
    me.greet((me.left, me.right, me.far))
    drain(down, down_sem)

    def product(t, base):
        rows = pl.ds(pl.multiple_of(t * 256, 256), 256)
        right = jnp.concatenate([down[0, :, columns(base + q * QUARTER, PART_BACK)] for q in range(2)], axis=1)
        both = jnp.dot(hidden[rows, :], right, preferred_element_type=jnp.float32)
        return both[:, :PART_BACK], both[:, PART_BACK:]

    def cross(i):
        base = me.base(UNITS_BACK + i)

        @pl.loop(0, 4)
        def _(t):
            core, z = t // 2, lax.rem(t, 2) * 2
            for q, own in enumerate(product(t, base)):
                across[i, q, core, pl.ds(z, 2)] = own.astype(jnp.bfloat16).reshape(2, 4, SLOTS, PART_BACK)

        for q, to in ((0, me.left), (1, me.right)):
            remote(across.at[i, q], crossed.at[i, q], cross_send.at[i], cross_recv.at[i], me.node, to)

    def send_rows(i):
        base = me.base(me.unit_of(i, SWAP_BACK))

        @pl.when(i < SWAP_BACK)
        def _():
            drain(crossed.at[i], cross_recv.at[i])

            @pl.loop(0, 4)
            def _(t):
                core, z = t // 2, lax.rem(t, 2) * 2
                for q, own in enumerate(product(t, base)):
                    other = crossed[i, q, core, pl.ds(z, 2)].reshape(256, PART_BACK).astype(jnp.float32)
                    outbound[i, q, core, pl.ds(z, 2)] = (
                        (own + other).astype(jnp.bfloat16).reshape(2, 4, SLOTS, PART_BACK)
                    )

        @pl.when(i >= SWAP_BACK)
        def _():
            @pl.loop(0, 4)
            def _(t):
                core, z = t // 2, lax.rem(t, 2) * 2
                for q, own in enumerate(product(t, base)):
                    outbound[i, q, core, pl.ds(z, 2)] = own.astype(jnp.bfloat16).reshape(2, 4, SLOTS, PART_BACK)

        for hops, other in PLACES:
            index, core, node = me.across(0, hops, other)
            remote(
                outbound.at[i, 0, core, :, index], plane.at[i, 0, me.y * 2 + me.core],
                send_sem.at[i], recv_sem.at[i], node, me.x,
            )
            index, core, node = me.across(1, hops, other)
            remote(
                outbound.at[i, 1, core, index], plane.at[i, 1, me.z * 2 + me.core],
                send_sem.at[i], recv_sem.at[i], node, me.x,
            )

        pltpu.make_async_copy(
            outbound.at[i, 0, me.core, :, me.y], plane.at[i, 0, me.y * 2 + me.core], recv_sem.at[i]
        ).start()
        pltpu.make_async_copy(
            outbound.at[i, 1, me.core, me.z], plane.at[i, 1, me.z * 2 + me.core], recv_sem.at[i]
        ).start()

    def send_sums(i):
        drain(plane.at[i], recv_sem.at[i])
        for q in range(2):
            for s in range(4):
                both = jnp.dot(
                    combine[q, s], plane[i, q, :, s].reshape(PLANE, PART_BACK), preferred_element_type=jnp.float32
                )
                sums[i, q, s] = (both[:TOK] + both[TOK:]).astype(jnp.bfloat16)
        for hops in HOPS:
            for q in range(2):
                index, node = me.along(q, hops)
                remote(
                    sums.at[i, q, index], gathered.at[i, q, me.own(q)], sum_send.at[i], sum_recv.at[i], node, me.x
                )
        for q in range(2):
            pltpu.make_async_copy(
                sums.at[i, q, me.own(q)], gathered.at[i, q, me.own(q)], sum_recv.at[i]
            ).start()

    def send_parts(i):
        drain(gathered.at[i], sum_recv.at[i])
        for q in range(2):
            whole[i, q] = (
                (gathered[i, q, 0].astype(jnp.float32) + gathered[i, q, 1].astype(jnp.float32))
                + (gathered[i, q, 2].astype(jnp.float32) + gathered[i, q, 3].astype(jnp.float32))
            ).astype(jnp.bfloat16)

        @pl.when(i < UNITS_BACK)
        def _():
            remote(whole.at[i, 1 - mine], partial.at[i, 0], part_send.at[i], part_recv.at[i, 0], me.node, me.far)

        @pl.when(i >= UNITS_BACK)
        def _():
            unit = i - UNITS_BACK + SWAP_BACK
            for q in range(2):
                owner = 1 - me.side + 2 * q
                slot = jnp.where(owner == me.right, 1, 2)
                remote(
                    whole.at[i, q], partial.at[unit, slot],
                    other_send.at[i - UNITS_BACK], part_recv.at[unit, slot], me.node, owner,
                )

    def finish(p):
        drain(partial.at[p, 0], part_recv.at[p, 0])
        value = whole[p, mine].astype(jnp.float32) + partial[p, 0].astype(jnp.float32)
        final[p] = value.astype(jnp.bfloat16)

        @pl.when(p >= SWAP_BACK)
        def _():
            for slot in (1, 2):
                drain(partial.at[p, slot], part_recv.at[p, slot])
            value = (whole[p, mine].astype(jnp.float32) + partial[p, 0].astype(jnp.float32)) + (
                partial[p, 1].astype(jnp.float32) + partial[p, 2].astype(jnp.float32)
            )
            final[p] = value.astype(jnp.bfloat16)

        cols = columns(me.side * HALF + mine * QUARTER + p * PART_BACK, PART_BACK)
        for to in (me.left, me.right, me.far):
            remote(final.at[p], out.at[:, cols], final_send.at[p], final_recv.at[p], me.node, to)
        out[:, cols] = final[p]

    def piece(o):
        return lax.rem(o + SWAP_BACK, straight)

    @pl.loop(-ROW_LEAD, straight + 2)
    def _(o):
        @pl.when((o >= 0) & (o < straight))
        def _():
            send_sums(piece(o))

        @pl.when(o + ROW_LEAD < straight)
        def _():
            send_rows(piece(o + ROW_LEAD))

        @pl.when(o + ROW_LEAD < SWAP_BACK)
        def _():
            cross(o + ROW_LEAD)

        @pl.when((o >= 1) & (o - 1 < straight))
        def _():
            send_parts(piece(o - 1))

        late = o - 2 - (straight - SWAP_BACK)

        @pl.when((late >= 0) & (late < SWAP_BACK))
        def _():
            finish(late)

        @pl.when((late >= LATE) & (late - LATE < UNITS_BACK - SWAP_BACK))
        def _():
            finish(SWAP_BACK + late - LATE)

    @pl.loop(0, straight)
    def _(i):
        drain(plane.at[i, :, pl.ds(0, 7)], send_sem.at[i])
        drain(gathered.at[i, :, pl.ds(0, 3)], sum_send.at[i])

    @pl.loop(0, SWAP_BACK)
    def _(i):
        drain(across.at[i], cross_send.at[i])

    @pl.loop(0, UNITS_BACK)
    def _(p):
        drain(whole.at[p, 0], part_send.at[p])
        drain(partial.at[p], final_send.at[p])
        drain(partial.at[p], final_recv.at[p])

    @pl.loop(0, UNITS_BACK - SWAP_BACK)
    def _(i):
        drain(whole.at[i], other_send.at[i])


def local(tokens, routes, route_weight, expert_gate, expert_up, expert_down):
    code = jnp.pad(
        ((routes << SHIFT) | route_weight).T, ((0, 0), (0, LANES - TOK)), constant_values=EXPERTS << SHIFT
    )

    vmem = pl.BlockSpec(memory_space=pltpu.VMEM)
    anywhere = pl.BlockSpec(memory_space=pl.ANY)
    dma = pltpu.SemaphoreType.DMA
    bf16 = jnp.bfloat16
    out_count, back_count = 2 * UNITS_OUT - SWAP_OUT, 2 * UNITS_BACK - SWAP_BACK
    by_source, by_plane = (2, 2, 4, 4, SLOTS), (2, 8, 4, SLOTS)
    hidden, combine = pl.pallas_call(
        dispatch_kernel,
        out_shape=(
            jax.ShapeDtypeStruct((ROWS, HID), bf16),
            jax.ShapeDtypeStruct((2, 4, 2 * TOK, PLANE), bf16),
        ),
        in_specs=[vmem, vmem, anywhere, anywhere],
        out_specs=(vmem, vmem),
        scratch_shapes=[
            pltpu.VMEM((2, 4, TOPK, LANES), jnp.int32),
            pltpu.VMEM((2, 4, PLANE, LANES), bf16),
            pltpu.VMEM((out_count, 2, 4, TOK, PART_OUT), bf16),
            pltpu.VMEM((out_count,) + by_plane + (PART_OUT,), bf16),
            pltpu.VMEM((out_count,) + by_source + (PART_OUT,), bf16),
            pltpu.VMEM((SWAP_OUT,) + by_source + (PART_OUT,), bf16),
            pltpu.VMEM((2 * UNITS_OUT, 2 * PART_OUT, 2 * HID), bf16),
            pltpu.VMEM((ROWS, 2 * HID), jnp.float32),
            dma(()), dma(()),
            dma((out_count,)), dma((out_count,)), dma((out_count,)), dma((out_count,)),
            dma((SWAP_OUT,)), dma((SWAP_OUT,)), dma((2 * UNITS_OUT,)),
        ],
        compiler_params=pltpu.CompilerParams(
            collective_id=0, has_side_effects=True, vmem_limit_bytes=56 * MIB
        ),
        name="dispatch",
    )(code, tokens, expert_gate, expert_up)
    return pl.pallas_call(
        return_kernel,
        out_shape=jax.ShapeDtypeStruct((TOK, D), bf16),
        in_specs=[vmem, anywhere, vmem],
        out_specs=vmem,
        scratch_shapes=[
            pltpu.VMEM((1, HID, D), bf16),
            pltpu.VMEM((SWAP_BACK,) + by_source + (PART_BACK,), bf16),
            pltpu.VMEM((SWAP_BACK,) + by_source + (PART_BACK,), bf16),
            pltpu.VMEM((back_count,) + by_source + (PART_BACK,), bf16),
            pltpu.VMEM((back_count,) + by_plane + (PART_BACK,), bf16),
            pltpu.VMEM((back_count, 2, 4, TOK, PART_BACK), bf16),
            pltpu.VMEM((back_count, 2, 4, TOK, PART_BACK), bf16),
            pltpu.VMEM((back_count, 2, TOK, PART_BACK), bf16),
            pltpu.VMEM((UNITS_BACK, 3, TOK, PART_BACK), bf16),
            pltpu.VMEM((UNITS_BACK, TOK, PART_BACK), bf16),
            dma((SWAP_BACK,)), dma((SWAP_BACK,)),
            dma((back_count,)), dma((back_count,)), dma((back_count,)), dma((back_count,)),
            dma((UNITS_BACK,)), dma((UNITS_BACK, 3)), dma((UNITS_BACK - SWAP_BACK,)), dma((UNITS_BACK,)), dma((UNITS_BACK,)), dma(()),
        ],
        compiler_params=pltpu.CompilerParams(
            collective_id=1, has_side_effects=True, vmem_limit_bytes=56 * MIB
        ),
        name="give_back",
    )(hidden, expert_down, combine)


def solution(mesh):
    return jax.shard_map(
        local,
        mesh=mesh,
        in_specs=(
            P("node", None),
            P("node", None),
            P("node", None),
            P("node", None, "local"),
            P("node", None, "local"),
            P("node", "local", None),
        ),
        out_specs=P("node", None),
        check_vma=False,
    )
```

```python
import jax
import jax.numpy as jnp
from jax import lax
from jax.experimental import pallas as pl
from jax.experimental.pallas import tpu as pltpu
from jax.sharding import PartitionSpec as P

EXPERTS = 32
SLOTS = 32
ROWS = 32 * SLOTS
D = 7168
HALF = D // 2
QUARTER = D // 4
HID = 512
TOK = 96
TOPK = 8
LANES = 128
UNITS_OUT = 14
UNITS_BACK = 7
PART_OUT = QUARTER // UNITS_OUT
PART_BACK = QUARTER // UNITS_BACK
SWAP_OUT = 10
SWAP_BACK = 5
PLANE = 8 * SLOTS
SHIFT = 11
STAGE_LEAD = 4
RELAY_LEAD = 2
PICK_LEAD = 2
ROW_LEAD = 2
LATE = 0
PASS_LAG = 10
HOPS = (1, 3, 2)
PLACES = ((1, 0), (3, 0), (2, 0), (1, 1), (3, 1), (2, 1), (0, 1))
MESH = pl.DeviceIdType.MESH
MIB = 1 << 20


def columns(start, size):
    return pl.ds(pl.multiple_of(start, size), size)


def drain(ref, sem):
    pltpu.make_async_copy(ref, ref, sem).wait()


def remote(src, dst, send_sem, recv_sem, node, x):
    pltpu.make_async_remote_copy(
        src_ref=src, dst_ref=dst, send_sem=send_sem, recv_sem=recv_sem,
        device_id=(node, x), device_id_type=MESH,
    ).start()


class Place:
    def __init__(self, units):
        self.units = units
        self.node, self.x = lax.axis_index("node"), lax.axis_index("local")
        self.core = lax.rem(self.node, 2)
        self.y = lax.rem(self.node // 2, 4)
        self.z = self.node // 8
        self.right, self.left = lax.rem(self.x + 1, 4), lax.rem(self.x + 3, 4)
        self.far = lax.rem(self.x + 2, 4)
        self.side = lax.rem(self.x, 2)

    def at(self, z, y, core):
        return (z * 4 + y) * 2 + core

    def turn(self, hops):
        return jnp.where(self.core == 0, hops, (4 - hops) % 4)

    def along(self, q, hops):
        if q == 0:
            index = lax.rem(self.z + self.turn(hops), 4)
            return index, self.at(index, self.y, self.core)
        index = lax.rem(self.y + self.turn(hops), 4)
        return index, self.at(self.z, index, self.core)

    def across(self, q, hops, other):
        core = self.core if other == 0 else 1 - self.core
        if q == 0:
            index = lax.rem(self.y + self.turn(hops), 4)
            return index, core, self.at(self.z, index, core)
        index = lax.rem(self.z + self.turn(hops), 4)
        return index, core, self.at(index, self.y, core)

    def own(self, q):
        return self.z if q == 0 else self.y

    def base(self, j):
        half = jnp.where(j < self.units, self.side, 1 - self.side)
        return half * HALF + lax.rem(j, self.units) * (QUARTER // self.units)

    def plane_experts(self, q):
        row = lax.broadcasted_iota(jnp.int32, (PLANE, LANES), 0)
        if q == 0:
            return (row >> 5) + self.z * 8, row & (SLOTS - 1)
        return (row >> 6) * 8 + self.y * 2 + ((row >> 5) & 1), row & (SLOTS - 1)

    def greet(self, others):
        barrier = pltpu.get_barrier_semaphore()

        def hello(node, x):
            pl.semaphore_signal(barrier, inc=1, device_id=(node, x), device_id_type=MESH)

        for hops, other in PLACES:
            hello(self.across(0, hops, other)[2], self.x)
            if hops:
                hello(self.across(1, hops, other)[2], self.x)
        for other in others:
            hello(self.node, other)
        pl.semaphore_wait(barrier, 13 + len(others))

    def unit_of(self, i, swapped):
        return jnp.where(i < self.units, i, i + swapped)


def dispatch_kernel(
    code, tokens, gate, up, hidden, combine,
    codes, select, staged, outbound, direct, passed, weights, total,
    code_send, code_recv, stage_send, stage_recv, relay_send, relay_recv, send_sem, recv_sem, pass_send, pass_recv, weight_sem,
):
    me = Place(UNITS_OUT)
    straight = direct.shape[0]

    me.greet((me.left, me.right))

    def stage(i):
        base = me.base(me.unit_of(i, SWAP_OUT))
        for hops in (1, 3):
            for q in range(2):
                remote(
                    tokens.at[:, columns(base + q * QUARTER, PART_OUT)], staged.at[i, q, me.own(q)],
                    stage_send.at[i], stage_recv.at[i], me.along(q, hops)[1], me.x,
                )
        for q in range(2):
            pltpu.make_async_copy(
                tokens.at[:, columns(base + q * QUARTER, PART_OUT)], staged.at[i, q, me.own(q)], stage_recv.at[i]
            ).start()

    def relay(i):
        drain(staged.at[i, :, pl.ds(0, 3)], stage_recv.at[i])
        for q in range(2):
            index = me.along(q, 3)[0]
            remote(
                staged.at[i, q, index], staged.at[i, q, index],
                relay_send.at[i], relay_recv.at[i], me.along(q, 1)[1], me.x,
            )

    for q in range(2):
        for hops in HOPS:
            remote(code, codes.at[q, me.own(q)], code_send, code_recv, me.along(q, hops)[1], me.x)
        pltpu.make_async_copy(code, codes.at[q, me.own(q)], code_recv).start()
    for i in range(STAGE_LEAD):
        stage(i)

    @pl.loop(0, 2 * UNITS_OUT)
    def _(j):
        for q in range(2):
            for m, source in enumerate((gate, up)):
                pltpu.make_async_copy(
                    source.at[0, columns(me.base(j) + q * QUARTER, PART_OUT)],
                    weights.at[j, pl.ds(q * PART_OUT, PART_OUT), pl.ds(m * HID, HID)],
                    weight_sem.at[j],
                ).start()

    drain(codes, code_recv)
    relay(0)
    lane = lax.broadcasted_iota(jnp.int32, (LANES, LANES), 1)
    earlier = (lax.broadcasted_iota(jnp.int32, (LANES, LANES), 0) < lane).astype(jnp.float32).astype(jnp.bfloat16)
    for q in range(2):
        expert, slot = me.plane_experts(q)
        for s in range(4):
            chosen = codes[q, s] >> SHIFT
            hit = chosen[0:1] == expert
            for k in range(1, TOPK):
                hit = hit | (chosen[k:k + 1] == expert)
            before = jnp.dot(
                hit.astype(jnp.float32).astype(jnp.bfloat16), earlier, preferred_element_type=jnp.float32
            )
            hit = hit & (before == slot.astype(jnp.float32))
            select[q, s] = hit.astype(jnp.float32).astype(jnp.bfloat16)

    def weigh():
        for q in range(2):
            expert, slot = me.plane_experts(q)
            for s in range(4):
                chosen = codes[q, s] >> SHIFT
                weight = codes[q, s] & ((1 << SHIFT) - 1)
                unit = jnp.where(chosen[0:1] == expert, weight[0:1], 0)
                for k in range(1, TOPK):
                    unit += jnp.where(chosen[k:k + 1] == expert, weight[k:k + 1], 0)
                unit = jnp.where(select[q, s].astype(jnp.float32) > 0.5, unit, 0)
                low = unit & 7
                for h, part in enumerate((unit - low, low)):
                    turned = jnp.transpose(part.astype(jnp.float32) * (1.0 / 1024.0))
                    combine[q, s, pl.ds(h * TOK, TOK)] = turned[:TOK].astype(jnp.bfloat16)

    def pick(i):
        drain(staged.at[i, :, 0], relay_recv.at[i])
        for q in range(2):
            for s in range(4):
                outbound[i, q, :, s] = jnp.dot(
                    select[q, s, :, :TOK], staged[i, q, s], preferred_element_type=jnp.float32
                ).astype(jnp.bfloat16).reshape(8, SLOTS, PART_OUT)

        for hops, other in PLACES:
            index, core, node = me.across(0, hops, other)
            remote(
                outbound.at[i, 0, index * 2 + core], direct.at[i, 0, me.core, :, me.y],
                send_sem.at[i], recv_sem.at[i], node, me.x,
            )
            index, core, node = me.across(1, hops, other)
            remote(
                outbound.at[i, 1, index * 2 + core], direct.at[i, 1, me.core, me.z],
                send_sem.at[i], recv_sem.at[i], node, me.x,
            )

        pltpu.make_async_copy(
            outbound.at[i, 0, me.y * 2 + me.core], direct.at[i, 0, me.core, :, me.y], recv_sem.at[i]
        ).start()
        pltpu.make_async_copy(
            outbound.at[i, 1, me.z * 2 + me.core], direct.at[i, 1, me.core, me.z], recv_sem.at[i]
        ).start()

    def add_product(rows_ref, i, j, first=False):
        drain(weights.at[j], weight_sem.at[j])

        @pl.loop(0, 4)
        def _(t):
            core, z = t // 2, lax.rem(t, 2) * 2
            rows = pl.ds(pl.multiple_of(t * 256, 256), 256)
            left = jnp.concatenate(
                [rows_ref[i, q, core, pl.ds(z, 2)].reshape(256, PART_OUT) for q in range(2)], axis=1
            )
            for m in range(2):
                cols = pl.ds(m * HID, HID)
                value = jnp.dot(left, weights[j, :, cols], preferred_element_type=jnp.float32)
                total[rows, cols] = value if first else total[rows, cols] + value

    def take_direct(i):
        drain(direct.at[i], recv_sem.at[i])

        @pl.when(i < SWAP_OUT)
        def _():
            for q, to in ((0, me.right), (1, me.left)):
                remote(direct.at[i, q], passed.at[i, q], pass_send.at[i], pass_recv.at[i], me.node, to)

        @pl.when(i == 0)
        def _():
            add_product(direct, i, me.unit_of(i, SWAP_OUT), first=True)

        @pl.when(i > 0)
        def _():
            add_product(direct, i, me.unit_of(i, SWAP_OUT))

    def take_passed(i):
        drain(passed.at[i], pass_recv.at[i])
        add_product(passed, i, UNITS_OUT + i)

    for i in range(1, RELAY_LEAD):
        relay(i)
    steps = max(straight + PICK_LEAD, SWAP_OUT + PASS_LAG)

    @pl.loop(0, steps)
    def _(i):
        @pl.when(i + STAGE_LEAD < straight)
        def _():
            stage(i + STAGE_LEAD)

        @pl.when(i + RELAY_LEAD < straight)
        def _():
            relay(i + RELAY_LEAD)

        @pl.when(i < straight)
        def _():
            pick(i)

        @pl.when(i == 2)
        def _():
            weigh()

        @pl.when((i >= PICK_LEAD) & (i - PICK_LEAD < straight))
        def _():
            take_direct(i - PICK_LEAD)

        @pl.when((i >= PASS_LAG) & (i - PASS_LAG < SWAP_OUT))
        def _():
            take_passed(i - PASS_LAG)

    @pl.loop(0, 4)
    def _(t):
        rows = pl.ds(pl.multiple_of(t * 256, 256), 256)
        g = total[rows, pl.ds(0, HID)]
        u = total[rows, pl.ds(HID, HID)]
        hidden[rows, :] = (g / (1.0 + jnp.exp(-g)) * u).astype(jnp.bfloat16)

    drain(codes.at[:, pl.ds(0, 3)], code_send)

    @pl.loop(0, straight)
    def _(i):
        drain(staged.at[i, :, pl.ds(0, 2)], stage_send.at[i])
        drain(staged.at[i, :, 0], relay_send.at[i])
        drain(outbound.at[i, :, pl.ds(0, 7)], send_sem.at[i])

    @pl.loop(0, SWAP_OUT)
    def _(i):
        drain(direct.at[i], pass_send.at[i])


def return_kernel(
    hidden, down_hbm, combine, out,
    down, across, crossed, outbound, plane, sums, gathered, whole, partial, final,
    cross_send, cross_recv, send_sem, recv_sem, sum_send, sum_recv,
    part_send, part_recv, other_send, final_send, final_recv, down_sem,
):
    me = Place(UNITS_BACK)
    straight = outbound.shape[0]
    mine = me.x // 2

    pltpu.make_async_copy(down_hbm, down, down_sem).start()
    me.greet((me.left, me.right, me.far))
    drain(down, down_sem)

    def product(t, base):
        rows = pl.ds(pl.multiple_of(t * 256, 256), 256)
        right = jnp.concatenate([down[0, :, columns(base + q * QUARTER, PART_BACK)] for q in range(2)], axis=1)
        both = jnp.dot(hidden[rows, :], right, preferred_element_type=jnp.float32)
        return both[:, :PART_BACK], both[:, PART_BACK:]

    def cross(i):
        base = me.base(UNITS_BACK + i)

        @pl.loop(0, 4)
        def _(t):
            core, z = t // 2, lax.rem(t, 2) * 2
            for q, own in enumerate(product(t, base)):
                across[i, q, core, pl.ds(z, 2)] = own.astype(jnp.bfloat16).reshape(2, 4, SLOTS, PART_BACK)

        for q, to in ((0, me.left), (1, me.right)):
            remote(across.at[i, q], crossed.at[i, q], cross_send.at[i], cross_recv.at[i], me.node, to)

    def send_rows(i):
        base = me.base(me.unit_of(i, SWAP_BACK))

        @pl.when(i < SWAP_BACK)
        def _():
            drain(crossed.at[i], cross_recv.at[i])

            @pl.loop(0, 4)
            def _(t):
                core, z = t // 2, lax.rem(t, 2) * 2
                for q, own in enumerate(product(t, base)):
                    other = crossed[i, q, core, pl.ds(z, 2)].reshape(256, PART_BACK).astype(jnp.float32)
                    outbound[i, q, core, pl.ds(z, 2)] = (
                        (own + other).astype(jnp.bfloat16).reshape(2, 4, SLOTS, PART_BACK)
                    )

        @pl.when(i >= SWAP_BACK)
        def _():
            @pl.loop(0, 4)
            def _(t):
                core, z = t // 2, lax.rem(t, 2) * 2
                for q, own in enumerate(product(t, base)):
                    outbound[i, q, core, pl.ds(z, 2)] = own.astype(jnp.bfloat16).reshape(2, 4, SLOTS, PART_BACK)

        for hops, other in PLACES:
            index, core, node = me.across(0, hops, other)
            remote(
                outbound.at[i, 0, core, :, index], plane.at[i, 0, me.y * 2 + me.core],
                send_sem.at[i], recv_sem.at[i], node, me.x,
            )
            index, core, node = me.across(1, hops, other)
            remote(
                outbound.at[i, 1, core, index], plane.at[i, 1, me.z * 2 + me.core],
                send_sem.at[i], recv_sem.at[i], node, me.x,
            )

        pltpu.make_async_copy(
            outbound.at[i, 0, me.core, :, me.y], plane.at[i, 0, me.y * 2 + me.core], recv_sem.at[i]
        ).start()
        pltpu.make_async_copy(
            outbound.at[i, 1, me.core, me.z], plane.at[i, 1, me.z * 2 + me.core], recv_sem.at[i]
        ).start()

    def send_sums(i):
        drain(plane.at[i], recv_sem.at[i])
        for q in range(2):
            for s in range(4):
                both = jnp.dot(
                    combine[q, s], plane[i, q, :, s].reshape(PLANE, PART_BACK), preferred_element_type=jnp.float32
                )
                sums[i, q, s] = (both[:TOK] + both[TOK:]).astype(jnp.bfloat16)
        for hops in HOPS:
            for q in range(2):
                index, node = me.along(q, hops)
                remote(
                    sums.at[i, q, index], gathered.at[i, q, me.own(q)], sum_send.at[i], sum_recv.at[i], node, me.x
                )
        for q in range(2):
            pltpu.make_async_copy(
                sums.at[i, q, me.own(q)], gathered.at[i, q, me.own(q)], sum_recv.at[i]
            ).start()

    def send_parts(i):
        drain(gathered.at[i], sum_recv.at[i])
        for q in range(2):
            whole[i, q] = (
                (gathered[i, q, 0].astype(jnp.float32) + gathered[i, q, 1].astype(jnp.float32))
                + (gathered[i, q, 2].astype(jnp.float32) + gathered[i, q, 3].astype(jnp.float32))
            ).astype(jnp.bfloat16)

        @pl.when(i < UNITS_BACK)
        def _():
            remote(whole.at[i, 1 - mine], partial.at[i, 0], part_send.at[i], part_recv.at[i, 0], me.node, me.far)

        @pl.when(i >= UNITS_BACK)
        def _():
            unit = i - UNITS_BACK + SWAP_BACK
            for q in range(2):
                owner = 1 - me.side + 2 * q
                slot = jnp.where(owner == me.right, 1, 2)
                remote(
                    whole.at[i, q], partial.at[unit, slot],
                    other_send.at[i - UNITS_BACK], part_recv.at[unit, slot], me.node, owner,
                )

    def finish(p):
        drain(partial.at[p, 0], part_recv.at[p, 0])
        value = whole[p, mine].astype(jnp.float32) + partial[p, 0].astype(jnp.float32)
        final[p] = value.astype(jnp.bfloat16)

        @pl.when(p >= SWAP_BACK)
        def _():
            for slot in (1, 2):
                drain(partial.at[p, slot], part_recv.at[p, slot])
            value = (whole[p, mine].astype(jnp.float32) + partial[p, 0].astype(jnp.float32)) + (
                partial[p, 1].astype(jnp.float32) + partial[p, 2].astype(jnp.float32)
            )
            final[p] = value.astype(jnp.bfloat16)

        cols = columns(me.side * HALF + mine * QUARTER + p * PART_BACK, PART_BACK)
        for to in (me.left, me.right, me.far):
            remote(final.at[p], out.at[:, cols], final_send.at[p], final_recv.at[p], me.node, to)
        out[:, cols] = final[p]

    def piece(o):
        return lax.rem(o + SWAP_BACK, straight)

    @pl.loop(-ROW_LEAD, straight + 2)
    def _(o):
        @pl.when((o >= 0) & (o < straight))
        def _():
            send_sums(piece(o))

        @pl.when(o + ROW_LEAD < SWAP_BACK)
        def _():
            cross(o + ROW_LEAD)

        @pl.when(o + ROW_LEAD < straight)
        def _():
            send_rows(piece(o + ROW_LEAD))

        @pl.when((o >= 1) & (o - 1 < straight))
        def _():
            send_parts(piece(o - 1))

        late = o - 2 - (straight - SWAP_BACK)

        @pl.when((late >= 0) & (late < SWAP_BACK))
        def _():
            finish(late)

        @pl.when((late >= LATE) & (late - LATE < UNITS_BACK - SWAP_BACK))
        def _():
            finish(SWAP_BACK + late - LATE)

    @pl.loop(0, straight)
    def _(i):
        drain(plane.at[i, :, pl.ds(0, 7)], send_sem.at[i])
        drain(gathered.at[i, :, pl.ds(0, 3)], sum_send.at[i])

    @pl.loop(0, SWAP_BACK)
    def _(i):
        drain(across.at[i], cross_send.at[i])

    @pl.loop(0, UNITS_BACK)
    def _(p):
        drain(whole.at[p, 0], part_send.at[p])
        drain(partial.at[p], final_send.at[p])
        drain(partial.at[p], final_recv.at[p])

    @pl.loop(0, UNITS_BACK - SWAP_BACK)
    def _(i):
        drain(whole.at[i], other_send.at[i])


def local(tokens, routes, route_weight, expert_gate, expert_up, expert_down):
    code = jnp.pad(
        ((routes << SHIFT) | route_weight).T, ((0, 0), (0, LANES - TOK)), constant_values=EXPERTS << SHIFT
    )

    vmem = pl.BlockSpec(memory_space=pltpu.VMEM)
    anywhere = pl.BlockSpec(memory_space=pl.ANY)
    dma = pltpu.SemaphoreType.DMA
    bf16 = jnp.bfloat16
    out_count, back_count = 2 * UNITS_OUT - SWAP_OUT, 2 * UNITS_BACK - SWAP_BACK
    by_source, by_plane = (2, 2, 4, 4, SLOTS), (2, 8, 4, SLOTS)
    hidden, combine = pl.pallas_call(
        dispatch_kernel,
        out_shape=(
            jax.ShapeDtypeStruct((ROWS, HID), bf16),
            jax.ShapeDtypeStruct((2, 4, 2 * TOK, PLANE), bf16),
        ),
        in_specs=[vmem, vmem, anywhere, anywhere],
        out_specs=(vmem, vmem),
        scratch_shapes=[
            pltpu.VMEM((2, 4, TOPK, LANES), jnp.int32),
            pltpu.VMEM((2, 4, PLANE, LANES), bf16),
            pltpu.VMEM((out_count, 2, 4, TOK, PART_OUT), bf16),
            pltpu.VMEM((out_count,) + by_plane + (PART_OUT,), bf16),
            pltpu.VMEM((out_count,) + by_source + (PART_OUT,), bf16),
            pltpu.VMEM((SWAP_OUT,) + by_source + (PART_OUT,), bf16),
            pltpu.VMEM((2 * UNITS_OUT, 2 * PART_OUT, 2 * HID), bf16),
            pltpu.VMEM((ROWS, 2 * HID), jnp.float32),
            dma(()), dma(()),
            dma((out_count,)), dma((out_count,)), dma((out_count,)), dma((out_count,)), dma((out_count,)), dma((out_count,)),
            dma((SWAP_OUT,)), dma((SWAP_OUT,)), dma((2 * UNITS_OUT,)),
        ],
        compiler_params=pltpu.CompilerParams(
            collective_id=0, has_side_effects=True, vmem_limit_bytes=56 * MIB
        ),
        name="dispatch",
    )(code, tokens, expert_gate, expert_up)
    return pl.pallas_call(
        return_kernel,
        out_shape=jax.ShapeDtypeStruct((TOK, D), bf16),
        in_specs=[vmem, anywhere, vmem],
        out_specs=vmem,
        scratch_shapes=[
            pltpu.VMEM((1, HID, D), bf16),
            pltpu.VMEM((SWAP_BACK,) + by_source + (PART_BACK,), bf16),
            pltpu.VMEM((SWAP_BACK,) + by_source + (PART_BACK,), bf16),
            pltpu.VMEM((back_count,) + by_source + (PART_BACK,), bf16),
            pltpu.VMEM((back_count,) + by_plane + (PART_BACK,), bf16),
            pltpu.VMEM((back_count, 2, 4, TOK, PART_BACK), bf16),
            pltpu.VMEM((back_count, 2, 4, TOK, PART_BACK), bf16),
            pltpu.VMEM((back_count, 2, TOK, PART_BACK), bf16),
            pltpu.VMEM((UNITS_BACK, 3, TOK, PART_BACK), bf16),
            pltpu.VMEM((UNITS_BACK, TOK, PART_BACK), bf16),
            dma((SWAP_BACK,)), dma((SWAP_BACK,)),
            dma((back_count,)), dma((back_count,)), dma((back_count,)), dma((back_count,)),
            dma((UNITS_BACK,)), dma((UNITS_BACK, 3)), dma((UNITS_BACK - SWAP_BACK,)), dma((UNITS_BACK,)), dma((UNITS_BACK,)), dma(()),
        ],
        compiler_params=pltpu.CompilerParams(
            collective_id=1, has_side_effects=True, vmem_limit_bytes=56 * MIB
        ),
        name="give_back",
    )(hidden, expert_down, combine)


def solution(mesh):
    return jax.shard_map(
        local,
        mesh=mesh,
        in_specs=(
            P("node", None),
            P("node", None),
            P("node", None),
            P("node", None, "local"),
            P("node", None, "local"),
            P("node", "local", None),
        ),
        out_specs=P("node", None),
        check_vma=False,
    )
```

```python
import jax
import jax.numpy as jnp
from jax import lax
from jax.experimental import pallas as pl
from jax.experimental.pallas import tpu as pltpu
from jax.sharding import PartitionSpec as P

EXPERTS = 32
SLOTS = 32
ROWS = 32 * SLOTS
D = 7168
HALF = D // 2
QUARTER = D // 4
HID = 512
TOK = 96
TOPK = 8
LANES = 128
UNITS_OUT = 14
UNITS_BACK = 7
PART_OUT = QUARTER // UNITS_OUT
PART_BACK = QUARTER // UNITS_BACK
SWAP_OUT = 10
SWAP_BACK = 5
PLANE = 8 * SLOTS
SHIFT = 11
STAGE_LEAD = 4
RELAY_LEAD = 2
PICK_LEAD = 2
ROW_LEAD = 2
LATE = 0
PASS_LAG = 10
HOPS = (1, 3, 2)
PLACES = ((1, 0), (3, 0), (2, 0), (1, 1), (3, 1), (2, 1), (0, 1))
MESH = pl.DeviceIdType.MESH
MIB = 1 << 20


def columns(start, size):
    return pl.ds(pl.multiple_of(start, size), size)


def drain(ref, sem):
    pltpu.make_async_copy(ref, ref, sem).wait()


def remote(src, dst, send_sem, recv_sem, node, x):
    pltpu.make_async_remote_copy(
        src_ref=src, dst_ref=dst, send_sem=send_sem, recv_sem=recv_sem,
        device_id=(node, x), device_id_type=MESH,
    ).start()


class Place:
    def __init__(self, units):
        self.units = units
        self.node, self.x = lax.axis_index("node"), lax.axis_index("local")
        self.core = lax.rem(self.node, 2)
        self.y = lax.rem(self.node // 2, 4)
        self.z = self.node // 8
        self.right, self.left = lax.rem(self.x + 1, 4), lax.rem(self.x + 3, 4)
        self.far = lax.rem(self.x + 2, 4)
        self.side = lax.rem(self.x, 2)

    def at(self, z, y, core):
        return (z * 4 + y) * 2 + core

    def turn(self, hops):
        return jnp.where(self.core == 0, hops, (4 - hops) % 4)

    def along(self, q, hops):
        if q == 0:
            index = lax.rem(self.z + self.turn(hops), 4)
            return index, self.at(index, self.y, self.core)
        index = lax.rem(self.y + self.turn(hops), 4)
        return index, self.at(self.z, index, self.core)

    def across(self, q, hops, other):
        core = self.core if other == 0 else 1 - self.core
        if q == 0:
            index = lax.rem(self.y + self.turn(hops), 4)
            return index, core, self.at(self.z, index, core)
        index = lax.rem(self.z + self.turn(hops), 4)
        return index, core, self.at(index, self.y, core)

    def own(self, q):
        return self.z if q == 0 else self.y

    def base(self, j):
        half = jnp.where(j < self.units, self.side, 1 - self.side)
        return half * HALF + lax.rem(j, self.units) * (QUARTER // self.units)

    def plane_experts(self, q):
        row = lax.broadcasted_iota(jnp.int32, (PLANE, LANES), 0)
        if q == 0:
            return (row >> 5) + self.z * 8, row & (SLOTS - 1)
        return (row >> 6) * 8 + self.y * 2 + ((row >> 5) & 1), row & (SLOTS - 1)

    def greet(self, others):
        barrier = pltpu.get_barrier_semaphore()

        def hello(node, x):
            pl.semaphore_signal(barrier, inc=1, device_id=(node, x), device_id_type=MESH)

        for hops, other in PLACES:
            hello(self.across(0, hops, other)[2], self.x)
            if hops:
                hello(self.across(1, hops, other)[2], self.x)
        for other in others:
            hello(self.node, other)
        pl.semaphore_wait(barrier, 13 + len(others))

    def unit_of(self, i, swapped):
        return jnp.where(i < self.units, i, i + swapped)


def dispatch_kernel(
    code, tokens, gate, up, hidden, combine,
    codes, select, staged, outbound, direct, passed, weights, total,
    code_send, code_recv, stage_send, stage_recv, relay_send, relay_recv, send_sem, recv_sem, pass_send, pass_recv, weight_sem,
):
    me = Place(UNITS_OUT)
    straight = direct.shape[0]

    me.greet((me.left, me.right))

    def stage(i):
        base = me.base(me.unit_of(i, SWAP_OUT))
        for hops in (1, 3):
            for q in range(2):
                remote(
                    tokens.at[:, columns(base + q * QUARTER, PART_OUT)], staged.at[i, q, me.own(q)],
                    stage_send.at[i], stage_recv.at[i], me.along(q, hops)[1], me.x,
                )
        for q in range(2):
            pltpu.make_async_copy(
                tokens.at[:, columns(base + q * QUARTER, PART_OUT)], staged.at[i, q, me.own(q)], stage_recv.at[i]
            ).start()

    def relay(i):
        drain(staged.at[i, :, pl.ds(0, 3)], stage_recv.at[i])
        for q in range(2):
            index = me.along(q, 3)[0]
            remote(
                staged.at[i, q, index], staged.at[i, q, index],
                relay_send.at[i], relay_recv.at[i], me.along(q, 1)[1], me.x,
            )

    for q in range(2):
        for hops in HOPS:
            remote(code, codes.at[q, me.own(q)], code_send, code_recv, me.along(q, hops)[1], me.x)
        pltpu.make_async_copy(code, codes.at[q, me.own(q)], code_recv).start()
    for i in range(STAGE_LEAD):
        stage(i)

    @pl.loop(0, 2 * UNITS_OUT)
    def _(j):
        for q in range(2):
            for m, source in enumerate((gate, up)):
                pltpu.make_async_copy(
                    source.at[0, columns(me.base(j) + q * QUARTER, PART_OUT)],
                    weights.at[j, pl.ds(q * PART_OUT, PART_OUT), pl.ds(m * HID, HID)],
                    weight_sem.at[j],
                ).start()

    drain(codes, code_recv)
    relay(0)
    lane = lax.broadcasted_iota(jnp.int32, (LANES, LANES), 1)
    earlier = (lax.broadcasted_iota(jnp.int32, (LANES, LANES), 0) < lane).astype(jnp.float32).astype(jnp.bfloat16)
    for q in range(2):
        expert, slot = me.plane_experts(q)
        for s in range(4):
            chosen = codes[q, s] >> SHIFT
            hit = chosen[0:1] == expert
            for k in range(1, TOPK):
                hit = hit | (chosen[k:k + 1] == expert)
            before = jnp.dot(
                hit.astype(jnp.float32).astype(jnp.bfloat16), earlier, preferred_element_type=jnp.float32
            )
            hit = hit & (before == slot.astype(jnp.float32))
            select[q, s] = hit.astype(jnp.float32).astype(jnp.bfloat16)

    def weigh():
        for q in range(2):
            expert, slot = me.plane_experts(q)
            for s in range(4):
                chosen = codes[q, s] >> SHIFT
                weight = codes[q, s] & ((1 << SHIFT) - 1)
                unit = jnp.where(chosen[0:1] == expert, weight[0:1], 0)
                for k in range(1, TOPK):
                    unit += jnp.where(chosen[k:k + 1] == expert, weight[k:k + 1], 0)
                unit = jnp.where(select[q, s].astype(jnp.float32) > 0.5, unit, 0)
                low = unit & 7
                for h, part in enumerate((unit - low, low)):
                    turned = jnp.transpose(part.astype(jnp.float32) * (1.0 / 1024.0))
                    combine[q, s, pl.ds(h * TOK, TOK)] = turned[:TOK].astype(jnp.bfloat16)

    def pick(i):
        drain(staged.at[i, :, 0], relay_recv.at[i])
        for q in range(2):
            for s in range(4):
                outbound[i, q, :, s] = jnp.dot(
                    select[q, s, :, :TOK], staged[i, q, s], preferred_element_type=jnp.float32
                ).astype(jnp.bfloat16).reshape(8, SLOTS, PART_OUT)

        for hops, other in PLACES:
            index, core, node = me.across(0, hops, other)
            remote(
                outbound.at[i, 0, index * 2 + core], direct.at[i, 0, me.core, :, me.y],
                send_sem.at[i], recv_sem.at[i], node, me.x,
            )
            index, core, node = me.across(1, hops, other)
            remote(
                outbound.at[i, 1, index * 2 + core], direct.at[i, 1, me.core, me.z],
                send_sem.at[i], recv_sem.at[i], node, me.x,
            )

        pltpu.make_async_copy(
            outbound.at[i, 0, me.y * 2 + me.core], direct.at[i, 0, me.core, :, me.y], recv_sem.at[i]
        ).start()
        pltpu.make_async_copy(
            outbound.at[i, 1, me.z * 2 + me.core], direct.at[i, 1, me.core, me.z], recv_sem.at[i]
        ).start()

    def add_product(rows_ref, i, j, first=False):
        drain(weights.at[j], weight_sem.at[j])

        @pl.loop(0, 4)
        def _(t):
            core, z = t // 2, lax.rem(t, 2) * 2
            rows = pl.ds(pl.multiple_of(t * 256, 256), 256)
            left = jnp.concatenate(
                [rows_ref[i, q, core, pl.ds(z, 2)].reshape(256, PART_OUT) for q in range(2)], axis=1
            )
            for m in range(2):
                cols = pl.ds(m * HID, HID)
                value = jnp.dot(left, weights[j, :, cols], preferred_element_type=jnp.float32)
                total[rows, cols] = value if first else total[rows, cols] + value

    def take_direct(i):
        drain(direct.at[i], recv_sem.at[i])

        @pl.when(i < SWAP_OUT)
        def _():
            for q, to in ((0, me.right), (1, me.left)):
                remote(direct.at[i, q], passed.at[i, q], pass_send.at[i], pass_recv.at[i], me.node, to)

        @pl.when(i == 0)
        def _():
            add_product(direct, i, me.unit_of(i, SWAP_OUT), first=True)

        @pl.when(i > 0)
        def _():
            add_product(direct, i, me.unit_of(i, SWAP_OUT))

    def take_passed(i):
        drain(passed.at[i], pass_recv.at[i])
        add_product(passed, i, UNITS_OUT + i)

    for i in range(1, RELAY_LEAD):
        relay(i)
    steps = max(straight + PICK_LEAD, SWAP_OUT + PASS_LAG)

    @pl.loop(0, steps)
    def _(i):
        @pl.when(i + STAGE_LEAD < straight)
        def _():
            stage(i + STAGE_LEAD)

        @pl.when(i + RELAY_LEAD < straight)
        def _():
            relay(i + RELAY_LEAD)

        @pl.when(i < straight)
        def _():
            pick(i)

        @pl.when(i == 10)
        def _():
            weigh()

        @pl.when((i >= PICK_LEAD) & (i - PICK_LEAD < straight))
        def _():
            take_direct(i - PICK_LEAD)

        @pl.when((i >= PASS_LAG) & (i - PASS_LAG < SWAP_OUT))
        def _():
            take_passed(i - PASS_LAG)

    @pl.loop(0, 4)
    def _(t):
        rows = pl.ds(pl.multiple_of(t * 256, 256), 256)
        g = total[rows, pl.ds(0, HID)]
        u = total[rows, pl.ds(HID, HID)]
        hidden[rows, :] = (g / (1.0 + jnp.exp(-g)) * u).astype(jnp.bfloat16)

    drain(codes.at[:, pl.ds(0, 3)], code_send)

    @pl.loop(0, straight)
    def _(i):
        drain(staged.at[i, :, pl.ds(0, 2)], stage_send.at[i])
        drain(staged.at[i, :, 0], relay_send.at[i])
        drain(outbound.at[i, :, pl.ds(0, 7)], send_sem.at[i])

    @pl.loop(0, SWAP_OUT)
    def _(i):
        drain(direct.at[i], pass_send.at[i])


def return_kernel(
    hidden, down_hbm, combine, out,
    down, across, crossed, outbound, plane, sums, gathered, whole, partial, final,
    cross_send, cross_recv, send_sem, recv_sem, sum_send, sum_recv,
    part_send, part_recv, other_send, final_send, final_recv, down_sem,
):
    me = Place(UNITS_BACK)
    straight = outbound.shape[0]
    mine = me.x // 2

    pltpu.make_async_copy(down_hbm, down, down_sem).start()
    me.greet((me.left, me.right, me.far))
    drain(down, down_sem)

    def product(t, base):
        rows = pl.ds(pl.multiple_of(t * 256, 256), 256)
        right = jnp.concatenate([down[0, :, columns(base + q * QUARTER, PART_BACK)] for q in range(2)], axis=1)
        both = jnp.dot(hidden[rows, :], right, preferred_element_type=jnp.float32)
        return both[:, :PART_BACK], both[:, PART_BACK:]

    def cross(i):
        base = me.base(UNITS_BACK + i)

        @pl.loop(0, 4)
        def _(t):
            core, z = t // 2, lax.rem(t, 2) * 2
            for q, own in enumerate(product(t, base)):
                across[i, q, core, pl.ds(z, 2)] = own.astype(jnp.bfloat16).reshape(2, 4, SLOTS, PART_BACK)

        for q, to in ((0, me.left), (1, me.right)):
            remote(across.at[i, q], crossed.at[i, q], cross_send.at[i], cross_recv.at[i], me.node, to)

    def send_rows(i):
        base = me.base(me.unit_of(i, SWAP_BACK))

        @pl.when(i < SWAP_BACK)
        def _():
            drain(crossed.at[i], cross_recv.at[i])

            @pl.loop(0, 4)
            def _(t):
                core, z = t // 2, lax.rem(t, 2) * 2
                for q, own in enumerate(product(t, base)):
                    other = crossed[i, q, core, pl.ds(z, 2)].reshape(256, PART_BACK).astype(jnp.float32)
                    outbound[i, q, core, pl.ds(z, 2)] = (
                        (own + other).astype(jnp.bfloat16).reshape(2, 4, SLOTS, PART_BACK)
                    )

        @pl.when(i >= SWAP_BACK)
        def _():
            @pl.loop(0, 4)
            def _(t):
                core, z = t // 2, lax.rem(t, 2) * 2
                for q, own in enumerate(product(t, base)):
                    outbound[i, q, core, pl.ds(z, 2)] = own.astype(jnp.bfloat16).reshape(2, 4, SLOTS, PART_BACK)

        for hops, other in PLACES:
            index, core, node = me.across(0, hops, other)
            remote(
                outbound.at[i, 0, core, :, index], plane.at[i, 0, me.y * 2 + me.core],
                send_sem.at[i], recv_sem.at[i], node, me.x,
            )
            index, core, node = me.across(1, hops, other)
            remote(
                outbound.at[i, 1, core, index], plane.at[i, 1, me.z * 2 + me.core],
                send_sem.at[i], recv_sem.at[i], node, me.x,
            )

        pltpu.make_async_copy(
            outbound.at[i, 0, me.core, :, me.y], plane.at[i, 0, me.y * 2 + me.core], recv_sem.at[i]
        ).start()
        pltpu.make_async_copy(
            outbound.at[i, 1, me.core, me.z], plane.at[i, 1, me.z * 2 + me.core], recv_sem.at[i]
        ).start()

    def send_sums(i):
        drain(plane.at[i], recv_sem.at[i])
        for q in range(2):
            for s in range(4):
                both = jnp.dot(
                    combine[q, s], plane[i, q, :, s].reshape(PLANE, PART_BACK), preferred_element_type=jnp.float32
                )
                sums[i, q, s] = (both[:TOK] + both[TOK:]).astype(jnp.bfloat16)
        for hops in HOPS:
            for q in range(2):
                index, node = me.along(q, hops)
                remote(
                    sums.at[i, q, index], gathered.at[i, q, me.own(q)], sum_send.at[i], sum_recv.at[i], node, me.x
                )
        for q in range(2):
            pltpu.make_async_copy(
                sums.at[i, q, me.own(q)], gathered.at[i, q, me.own(q)], sum_recv.at[i]
            ).start()

    def send_parts(i):
        drain(gathered.at[i], sum_recv.at[i])
        for q in range(2):
            whole[i, q] = (
                (gathered[i, q, 0].astype(jnp.float32) + gathered[i, q, 1].astype(jnp.float32))
                + (gathered[i, q, 2].astype(jnp.float32) + gathered[i, q, 3].astype(jnp.float32))
            ).astype(jnp.bfloat16)

        @pl.when(i < UNITS_BACK)
        def _():
            remote(whole.at[i, 1 - mine], partial.at[i, 0], part_send.at[i], part_recv.at[i, 0], me.node, me.far)

        @pl.when(i >= UNITS_BACK)
        def _():
            unit = i - UNITS_BACK + SWAP_BACK
            for q in range(2):
                owner = 1 - me.side + 2 * q
                slot = jnp.where(owner == me.right, 1, 2)
                remote(
                    whole.at[i, q], partial.at[unit, slot],
                    other_send.at[i - UNITS_BACK], part_recv.at[unit, slot], me.node, owner,
                )

    def finish(p):
        drain(partial.at[p, 0], part_recv.at[p, 0])
        value = whole[p, mine].astype(jnp.float32) + partial[p, 0].astype(jnp.float32)
        final[p] = value.astype(jnp.bfloat16)

        @pl.when(p >= SWAP_BACK)
        def _():
            for slot in (1, 2):
                drain(partial.at[p, slot], part_recv.at[p, slot])
            value = (whole[p, mine].astype(jnp.float32) + partial[p, 0].astype(jnp.float32)) + (
                partial[p, 1].astype(jnp.float32) + partial[p, 2].astype(jnp.float32)
            )
            final[p] = value.astype(jnp.bfloat16)

        cols = columns(me.side * HALF + mine * QUARTER + p * PART_BACK, PART_BACK)
        for to in (me.left, me.right, me.far):
            remote(final.at[p], out.at[:, cols], final_send.at[p], final_recv.at[p], me.node, to)
        out[:, cols] = final[p]

    def piece(o):
        return lax.rem(o + SWAP_BACK, straight)

    @pl.loop(-ROW_LEAD, straight + 2)
    def _(o):
        @pl.when((o >= 0) & (o < straight))
        def _():
            send_sums(piece(o))

        @pl.when(o + ROW_LEAD < SWAP_BACK)
        def _():
            cross(o + ROW_LEAD)

        @pl.when(o + ROW_LEAD < straight)
        def _():
            send_rows(piece(o + ROW_LEAD))

        @pl.when((o >= 1) & (o - 1 < straight))
        def _():
            send_parts(piece(o - 1))

        late = o - 2 - (straight - SWAP_BACK)

        @pl.when((late >= 0) & (late < SWAP_BACK))
        def _():
            finish(late)

        @pl.when((late >= LATE) & (late - LATE < UNITS_BACK - SWAP_BACK))
        def _():
            finish(SWAP_BACK + late - LATE)

    @pl.loop(0, straight)
    def _(i):
        drain(plane.at[i, :, pl.ds(0, 7)], send_sem.at[i])
        drain(gathered.at[i, :, pl.ds(0, 3)], sum_send.at[i])

    @pl.loop(0, SWAP_BACK)
    def _(i):
        drain(across.at[i], cross_send.at[i])

    @pl.loop(0, UNITS_BACK)
    def _(p):
        drain(whole.at[p, 0], part_send.at[p])
        drain(partial.at[p], final_send.at[p])
        drain(partial.at[p], final_recv.at[p])

    @pl.loop(0, UNITS_BACK - SWAP_BACK)
    def _(i):
        drain(whole.at[i], other_send.at[i])


def local(tokens, routes, route_weight, expert_gate, expert_up, expert_down):
    code = jnp.pad(
        ((routes << SHIFT) | route_weight).T, ((0, 0), (0, LANES - TOK)), constant_values=EXPERTS << SHIFT
    )

    vmem = pl.BlockSpec(memory_space=pltpu.VMEM)
    anywhere = pl.BlockSpec(memory_space=pl.ANY)
    dma = pltpu.SemaphoreType.DMA
    bf16 = jnp.bfloat16
    out_count, back_count = 2 * UNITS_OUT - SWAP_OUT, 2 * UNITS_BACK - SWAP_BACK
    by_source, by_plane = (2, 2, 4, 4, SLOTS), (2, 8, 4, SLOTS)
    hidden, combine = pl.pallas_call(
        dispatch_kernel,
        out_shape=(
            jax.ShapeDtypeStruct((ROWS, HID), bf16),
            jax.ShapeDtypeStruct((2, 4, 2 * TOK, PLANE), bf16),
        ),
        in_specs=[vmem, vmem, anywhere, anywhere],
        out_specs=(vmem, vmem),
        scratch_shapes=[
            pltpu.VMEM((2, 4, TOPK, LANES), jnp.int32),
            pltpu.VMEM((2, 4, PLANE, LANES), bf16),
            pltpu.VMEM((out_count, 2, 4, TOK, PART_OUT), bf16),
            pltpu.VMEM((out_count,) + by_plane + (PART_OUT,), bf16),
            pltpu.VMEM((out_count,) + by_source + (PART_OUT,), bf16),
            pltpu.VMEM((SWAP_OUT,) + by_source + (PART_OUT,), bf16),
            pltpu.VMEM((2 * UNITS_OUT, 2 * PART_OUT, 2 * HID), bf16),
            pltpu.VMEM((ROWS, 2 * HID), jnp.float32),
            dma(()), dma(()),
            dma((out_count,)), dma((out_count,)), dma((out_count,)), dma((out_count,)), dma((out_count,)), dma((out_count,)),
            dma((SWAP_OUT,)), dma((SWAP_OUT,)), dma((2 * UNITS_OUT,)),
        ],
        compiler_params=pltpu.CompilerParams(
            collective_id=0, has_side_effects=True, vmem_limit_bytes=56 * MIB
        ),
        name="dispatch",
    )(code, tokens, expert_gate, expert_up)
    return pl.pallas_call(
        return_kernel,
        out_shape=jax.ShapeDtypeStruct((TOK, D), bf16),
        in_specs=[vmem, anywhere, vmem],
        out_specs=vmem,
        scratch_shapes=[
            pltpu.VMEM((1, HID, D), bf16),
            pltpu.VMEM((SWAP_BACK,) + by_source + (PART_BACK,), bf16),
            pltpu.VMEM((SWAP_BACK,) + by_source + (PART_BACK,), bf16),
            pltpu.VMEM((back_count,) + by_source + (PART_BACK,), bf16),
            pltpu.VMEM((back_count,) + by_plane + (PART_BACK,), bf16),
            pltpu.VMEM((back_count, 2, 4, TOK, PART_BACK), bf16),
            pltpu.VMEM((back_count, 2, 4, TOK, PART_BACK), bf16),
            pltpu.VMEM((back_count, 2, TOK, PART_BACK), bf16),
            pltpu.VMEM((UNITS_BACK, 3, TOK, PART_BACK), bf16),
            pltpu.VMEM((UNITS_BACK, TOK, PART_BACK), bf16),
            dma((SWAP_BACK,)), dma((SWAP_BACK,)),
            dma((back_count,)), dma((back_count,)), dma((back_count,)), dma((back_count,)),
            dma((UNITS_BACK,)), dma((UNITS_BACK, 3)), dma((UNITS_BACK - SWAP_BACK,)), dma((UNITS_BACK,)), dma((UNITS_BACK,)), dma(()),
        ],
        compiler_params=pltpu.CompilerParams(
            collective_id=1, has_side_effects=True, vmem_limit_bytes=56 * MIB
        ),
        name="give_back",
    )(hidden, expert_down, combine)


def solution(mesh):
    return jax.shard_map(
        local,
        mesh=mesh,
        in_specs=(
            P("node", None),
            P("node", None),
            P("node", None),
            P("node", None, "local"),
            P("node", None, "local"),
            P("node", "local", None),
        ),
        out_specs=P("node", None),
        check_vma=False,
    )
```
